512 devices in a mesh: band: 8 (over z_hi, core), tile: 64 (over x, y, z_lo).
Axes of the slice: x: 4, y: 8, z: 8 (z_hi: 4, z_lo: 2; z = z_hi * 2 + z_lo), core: 2. Of those that a mesh axis runs over, the one named last changes fastest.
Arguments:
- waveforms: bfloat16 [2048, 32, 500], P('tile', 'band'), may hold values from -6 to 6
- band_widths: int32 [8], replicated, may hold values from 1 to 34, 180 in all
- pair_table: int32 [64, 33], P('tile'), may hold values from 0 to 63, as said below
Outputs:
- correlations: bfloat16 [64, 33, 32, 32, 51], P('tile', None, 'band')
The draws below stay inside these ranges and needn't reach their ends.
Inputs may be any that keep to these rules, and one draw needn't show every extreme that they name: `band_widths`: the widths sum to 180; the largest is exactly 34. `pair_table`: row t lists the blocks t, t - 1, ..., t - 33 + 1 modulo 64, each once, in some order.
All inputs are finite; a program needn't handle non-finite values.
Results may differ from the reference program's by a relative error of at most 0.018.
Values may be sent and summed in bfloat16 or wider, within the bound.
A program may use at most 192 MiB of HBM per device.

```python
import math
import jax
import jax.numpy as jnp
import numpy as np
from jax import lax

BLOCK = 32
SEG = 32
SAMPLES = 500
BINS = 180
FIRST = 20
LAGS = 51
CAP = 34
CHANNELS = 2048
SLOTS = 33
N_BAND = 8
N_TILE = 64


def draw_pair_table(key, part):
    key = jax.random.fold_in(key, 7)
    row_keys = jax.random.split(key, N_TILE)
    orders = jax.vmap(lambda row_key: jax.random.permutation(row_key, SLOTS))(row_keys)
    owners = jnp.arange(N_TILE, dtype=jnp.int32)[:, None]
    return ((owners + N_TILE - orders.astype(jnp.int32)) % N_TILE).astype(jnp.int32)


def level_of(key, dims, cuts, low, largest):
    factor_of = 1.0
    for dim, shards_of in cuts:
        steps = jax.random.uniform(jax.random.fold_in(jax.random.fold_in(key, 6), dim), (shards_of,), jnp.float32, low / len(cuts), largest / len(cuts))
        factor_of = factor_of * jnp.repeat(jnp.exp(steps), dims[dim] // shards_of).reshape((-1,) + (1,) * (len(dims) - 1 - dim))
    return factor_of


def profile(amount, total, most, lean):
    loads = [(1 << 20) // math.isqrt(grade ** lean) + 1 for grade in range(2, amount + 1)]
    surplus, given = total - most - (amount - 1), [1] * (amount - 1)
    while surplus > 0:
        movable = [i for i in range(amount - 1) if given[i] < most]
        pool, budget = sum([loads[i] for i in movable]), surplus
        for i in movable:
            addition = min(most - given[i], max(1, budget * loads[i] // pool), surplus)
            given[i] = given[i] + addition
            surplus = surplus - addition
    return np.array([most] + given)


def ragged_sizes(stream_key, number_of, total, most, slope):
    if number_of == 2:
        one = jax.random.randint(stream_key, (), max(1, total - most), min(most, total - 1) + 1)
        return jnp.stack([one, total - one])
    lengths = jnp.asarray(profile(number_of, total, most, slope), jnp.int32)
    couples = (number_of - 1) // 2
    donor, taker = lengths[1:1 + 2 * couples:2], lengths[2:2 + 2 * couples:2]
    margin = jnp.minimum(donor - 1, most - taker)
    shifted = jax.random.randint(jax.random.fold_in(stream_key, 1), (couples,), 0, 1 << 20) % (margin + 1)
    lengths = lengths.at[1:1 + 2 * couples:2].set(donor - shifted).at[2:2 + 2 * couples:2].set(taker + shifted)
    return lengths[jax.random.permutation(jax.random.fold_in(stream_key, 2), number_of)]


def gaussian(own_key, shape, deviation, reach, cuts=(), held_as=jnp.bfloat16):
    entries = deviation * jax.random.normal(own_key, shape, jnp.float32)
    if cuts:
        entries = entries * level_of(own_key, shape, cuts, -0.22, 0.18)
    return jnp.clip(entries, -reach, reach).astype(held_as)


def setup_inputs(seed: int = 0) -> dict:
    splits = jax.random.split(jax.random.key(seed), 4)
    return {
        "waveforms": gaussian(splits[0], (CHANNELS, SEG, SAMPLES), 1.0, 6.0, ((0, 64), (1, 8))),
        "band_widths": ragged_sizes(splits[1], N_BAND, BINS, CAP, 2).astype(jnp.int32),
        "pair_table": draw_pair_table(jax.random.fold_in(splits[3], 71), 0),
    }


EPS = 1e-05

def slot_bins(band_widths):
    offsets = jnp.cumsum(band_widths) - band_widths
    slot_ids = jnp.arange(CAP, dtype=jnp.int32)
    bin_freq = (FIRST + offsets[:, None] + slot_ids[None, :]).astype(jnp.int32)
    in_band = (slot_ids[None, :] < band_widths[:, None]).astype(jnp.float32)
    return (bin_freq, in_band)

def forward_table(bin_freq, in_band):
    sample_ids = jnp.arange(SAMPLES, dtype=jnp.int32)
    phase_ids = sample_ids[:, None, None] * bin_freq[None] % SAMPLES
    angles = phase_ids.astype(jnp.float32) * (2.0 * math.pi / SAMPLES)
    weight = in_band[None]
    return jnp.stack([jnp.cos(angles) * weight, -jnp.sin(angles) * weight], axis=2).astype(jnp.bfloat16)

def inverse_table(bin_freq, in_band):
    lag_ids = jnp.arange(LAGS, dtype=jnp.int32) - LAGS // 2
    phase_ids = bin_freq[:, :, None] * lag_ids[None, None, :] % SAMPLES
    angles = phase_ids.astype(jnp.float32) * (2.0 * math.pi / SAMPLES)
    weight = in_band[:, :, None]
    return jnp.stack([jnp.cos(angles) * weight, -jnp.sin(angles) * weight], axis=1).astype(jnp.bfloat16)

def reference(waveforms, band_widths, pair_table):
    bin_freq, in_band = slot_bins(band_widths)
    forward = forward_table(bin_freq, in_band).reshape(SAMPLES, N_BAND * 2 * CAP)
    spectra = jnp.dot(waveforms.reshape(CHANNELS * SEG, SAMPLES), forward, preferred_element_type=jnp.float32)
    spectra = spectra.astype(jnp.bfloat16).reshape(CHANNELS, SEG, N_BAND, 2, CAP).astype(jnp.float32)
    energy = lax.optimization_barrier(jnp.sum(spectra * spectra, axis=(1, 3, 4))) / (SEG * band_widths.astype(jnp.float32))
    gain = lax.rsqrt(energy + EPS)
    whitened = (spectra * gain[:, None, :, None, None]).astype(jnp.bfloat16)
    blocks = whitened.reshape(N_TILE, BLOCK, SEG, N_BAND, 2, CAP)
    inverse = inverse_table(bin_freq, in_band).astype(jnp.float32)
    scale_out = 1.0 / math.sqrt(SEG * BINS)

    def owner_lags(inputs):
        own_block, partners = inputs
        own_float = own_block.astype(jnp.float32)
        other_float = jnp.take(blocks, partners, axis=0).astype(jnp.float32)
        real_part = jnp.einsum('isbpq,tjsbpq->tbijq', own_float, other_float)
        imag_part = jnp.einsum('isbq,tjsbq->tbijq', own_float[:, :, :, 1], other_float[:, :, :, :, 0])
        imag_part = imag_part - jnp.einsum('isbq,tjsbq->tbijq', own_float[:, :, :, 0], other_float[:, :, :, :, 1])
        cross_spec = jnp.stack([real_part, imag_part], axis=4)
        cross_spec = lax.optimization_barrier(cross_spec.astype(jnp.bfloat16)).astype(jnp.float32)
        band_lags = jnp.einsum('tbijpq,bpql->tbijl', cross_spec, inverse) * scale_out
        band_lags = lax.optimization_barrier(band_lags.astype(jnp.bfloat16)).astype(jnp.float32)
        return lax.optimization_barrier(jnp.sum(band_lags, axis=1)).astype(jnp.bfloat16)
    return lax.map(owner_lags, (blocks, pair_table))
```

```python
import functools
import math

import jax
import jax.numpy as jnp
import ml_dtypes
import numpy as np
from jax import lax
from jax.experimental import pallas as pl
from jax.experimental.pallas import tpu as pltpu
from jax.sharding import PartitionSpec as P

BINS = 180
FIRST = 20
LAGS = 51
SAMPLES = 500
EPS = 1e-05

BAND = 8
TILE = 64
CH = 32
SEG = 32
SEGL = 4
QN = 24
GROUPS = QN // 4
ROWS = 2 * QN
WIDE = QN * 64
PART = 208
HALF_A = 112
SCALE = 1.0 / math.sqrt(SEG * BINS)
MESH = pl.DeviceIdType.MESH

ORDER = [0, 8, 16, 1, 9, 7, 15, 2, 10, 6, 14, 3, 11, 5, 13, 4, 12]
POS = {r: i for i, r in enumerate(ORDER)}
CHUNKS = [(0, 256), (256, 256), (512, 256), (768, 256), (1024, 128)]
JALL = 1152


def _forward_const():
    n = np.arange(SAMPLES)
    table = np.zeros((BAND * QN, 2, 512), np.float32)
    for k in range(BINS):
        angle = ((n * (FIRST + k)) % SAMPLES) * (2.0 * math.pi / SAMPLES)
        table[k, 0, :SAMPLES] = np.cos(angle)
        table[k, 1, :SAMPLES] = -np.sin(angle)
    return table.reshape(BAND * ROWS, 512).astype(ml_dtypes.bfloat16)


def _inverse_const():
    tau = np.arange(LAGS) - LAGS // 2
    table = np.zeros((BAND * QN, 2, LAGS), np.float32)
    for k in range(BINS):
        angle = (((FIRST + k) * tau) % SAMPLES) * (2.0 * math.pi / SAMPLES)
        table[k, 0] = np.cos(angle)
        table[k, 1] = -np.sin(angle)
    table = table.reshape(BAND, GROUPS, 4, 2, LAGS)
    out = np.zeros((BAND, 4, PART, GROUPS, 4, 2, 16), np.float32)
    for b4 in range(4):
        for i4 in range(4):
            rows = np.moveaxis(table, -1, 1)
            out[:, b4, i4 * LAGS : (i4 + 1) * LAGS, :, :, :, b4 * 4 + i4] = rows
    return out.reshape(BAND, 4 * PART, GROUPS * 128).astype(ml_dtypes.bfloat16)


def _select_const():
    out = np.zeros((PART, 512), np.float32)
    for i4 in range(4):
        for lag in range(LAGS):
            out[i4 * LAGS + lag, i4 * 128 + lag] = 1.0
    return out.astype(ml_dtypes.bfloat16)


def _main_kernel(widths, wave, fwd, inv_all, out, *scratch):
    sb, rb, g, wt, kt, ct = scratch[:6]
    bufs = [scratch[6 + 6 * k : 12 + 6 * k] for k in range(len(CHUNKS))]
    (kt_sem, a_send, a_recv, g_send, g_recv, r_send, r_recv) = scratch[6 + 6 * len(CHUNKS) :]
    f32, bf16 = jnp.float32, jnp.bfloat16

    band = lax.axis_index("band")
    tile = lax.axis_index("tile")
    core = lax.rem(band, 2)
    zh = band // 2
    z = lax.rem(tile, 2)

    def at_band(b):
        return {"band": b, "tile": tile}

    def at_tile(t):
        return {"band": band, "tile": lax.rem(t + TILE, TILE)}

    barrier = pltpu.get_barrier_semaphore()
    peers = [at_band(lax.rem(band + o, BAND)) for o in range(1, BAND)]
    other_z = tile + 1 - 2 * z
    peers += [at_tile(other_z)] + [at_tile(tile + d) for d in (16, -16, 32, 2, -2)]
    for peer in peers:
        pl.semaphore_signal(barrier, inc=1, device_id=peer, device_id_type=MESH)
    kt_copy = pltpu.make_async_copy(inv_all.at[band], kt, kt_sem)
    kt_copy.start()

    nt = (((1,), (1,)), ((), ()))
    spectra = lax.dot_general(fwd[...], wave[...], nt, preferred_element_type=f32).astype(bf16)
    values = spectra.astype(f32)
    squares = values * values
    sq_hi = squares.astype(bf16)
    sq_lo = (squares - sq_hi.astype(f32)).astype(bf16)
    offsets = []
    total = widths[0] * 0
    for b in range(BAND):
        offsets.append(total)
        total = total + widths[b]

    def member(rows, bins):
        low = jnp.zeros(rows.shape, jnp.int32)
        size = jnp.zeros(rows.shape, jnp.int32)
        for b in range(BAND):
            low = jnp.where(rows == b, offsets[b], low)
            size = jnp.where(rows == b, widths[b], size)
        return jnp.where((bins >= low) & (bins < low + size), 1.0, 0.0).astype(f32)

    shape = (BAND, BAND * ROWS)
    is_in = member(
        lax.broadcasted_iota(jnp.int32, shape, 0), lax.broadcasted_iota(jnp.int32, shape, 1) // 2
    ).astype(bf16)
    part = jnp.dot(is_in, sq_hi, preferred_element_type=f32)
    part = part + jnp.dot(is_in, sq_lo, preferred_element_type=f32)
    part_hi = part.astype(bf16).astype(f32)
    energies = jnp.concatenate([part_hi, part - part_hi], axis=0).astype(bf16)
    for b in range(BAND):
        sb[b, :ROWS] = spectra[b * ROWS : (b + 1) * ROWS]
        sb[b, ROWS:] = energies
    g[1088:, :] = jnp.zeros((JALL - 1088, WIDE), bf16)
    rb[0] = sb[band]

    pl.semaphore_wait(barrier, len(peers))

    exchange = []
    for o in range(1, BAND):
        to = lax.rem(band + o, BAND)
        copy = pltpu.make_async_remote_copy(
            src_ref=sb.at[to],
            dst_ref=rb.at[o],
            send_sem=a_send.at[o],
            recv_sem=a_recv.at[o],
            device_id=at_band(to),
            device_id_type=MESH,
        )
        copy.start()
        exchange.append(copy)
    for copy in exchange:
        copy.wait_recv()

    energy = jnp.zeros((BAND, 128), f32)
    for o in range(BAND):
        tail = rb[o, ROWS:].astype(f32)
        energy = energy + tail[:BAND] + tail[BAND:]
    energy = energy + pltpu.roll(energy, 64, 1)
    energy = energy + pltpu.roll(energy, 32, 1)
    row8 = lax.broadcasted_iota(jnp.int32, (BAND, 128), 0)
    width8 = jnp.ones((BAND, 128), f32)
    for b in range(BAND):
        width8 = jnp.where(row8 == b, widths[b].astype(f32), width8)
    gain = lax.rsqrt(energy / (SEG * width8) + EPS)
    bins = band * QN + lax.broadcasted_iota(jnp.int32, (ROWS, 128), 0) // 2
    gains = jnp.zeros((ROWS, 128), f32)
    for b in range(BAND):
        inside = (bins >= offsets[b]) & (bins < offsets[b] + widths[b])
        gains = jnp.where(inside, gain[b : b + 1, :], gains)
    white = [(rb[o, :ROWS].astype(f32) * gains).astype(bf16).astype(f32) for o in range(BAND)]

    lane = lax.broadcasted_iota(jnp.int32, (CH, 128), 1)
    own_row = pl.multiple_of(z * CH, CH)
    tiles = []
    for pair in range(GROUPS // 2):
        stack = jnp.concatenate(
            [white[o][(2 * pair + h) * 8 : (2 * pair + h + 1) * 8] for h in range(2) for o in range(BAND)],
            axis=0,
        )
        flipped = jnp.transpose(stack)
        rolled = pltpu.roll(flipped, 64, 1)
        seg = [flipped[s * CH : (s + 1) * CH] for s in range(SEGL)]
        seg_r = [rolled[s * CH : (s + 1) * CH] for s in range(SEGL)]
        for h in range(2):
            low, high = (seg, seg_r) if h == 0 else (seg_r, seg)
            halves = [jnp.where(lane < 64, low[2 * v], high[2 * v + 1]) for v in range(2)]
            tiles.append(halves)
            base = (2 * pair + h) * 256
            for v in range(2):
                g[pl.ds(own_row, CH), base + v * 128 : base + (v + 1) * 128] = halves[v].astype(bf16)

    def slot(r, half=None):
        if half is None:
            return g.at[pl.ds(POS[r] * 64, 64)]
        return g.at[pl.ds(pl.multiple_of(POS[r] * 64 + half * CH, CH), CH)]

    copies = {}

    def move(name, src, dst, to):
        n = len(copies)
        copy = pltpu.make_async_remote_copy(
            src_ref=src,
            dst_ref=dst,
            send_sem=g_send.at[n],
            recv_sem=g_recv.at[n],
            device_id=at_tile(to),
            device_id_type=MESH,
        )
        copy.start()
        copies[name] = copy

    move("z", slot(0, z), slot(0, z), other_z)
    move("x1", slot(0, z), slot(8, z), tile + 16)
    move("x2", slot(0, z), slot(16, z), tile + 32)

    even = lax.rem(lane, 2) == 0
    bin4 = lax.rem(lane // 2, 4)
    for n, halves in enumerate(tiles):
        for v in range(2):
            own = halves[v]
            alt = jnp.where(even, pltpu.roll(own, 127, 1), -pltpu.roll(own, 1, 1))
            for q in range(4):
                for p in range(2):
                    kept = jnp.where(bin4 == q, own if p == 0 else alt, 0.0).astype(bf16)
                    for h in range(2):
                        row = h * 128 + q * 32 + p * 16
                        wt[n, row : row + 16, v * 128 : (v + 1) * 128] = kept[h * 16 : h * 16 + 16]

    def forward(kind, k):
        if kind == "fa":
            src, dst, to = k - 1, k, tile + 2
        elif kind == "fb":
            src, dst, to = 8 + k - 1, 8 + k, tile + 2
        elif kind == "ba":
            src, dst, to = 8 - (k - 1), 8 - k, tile - 2
        else:
            src, dst, to = 16 - (k - 1), 16 - k, tile - 2
        move(kind + str(k), slot(src), slot(dst), to)

    def arrive(kind, k, last):
        copies[kind + str(k)].wait_recv()
        if k < last:
            forward(kind, k + 1)

    copies["z"].wait_recv()
    move("x1s", slot(0, 1 - z), slot(8, 1 - z), tile + 16)
    move("x2s", slot(0, 1 - z), slot(16, 1 - z), tile + 32)
    forward("fa", 1)
    copies["x1"].wait_recv()
    copies["x1s"].wait_recv()
    forward("ba", 1)
    forward("fb", 1)
    copies["x2"].wait_recv()
    copies["x2s"].wait_recv()
    forward("bb", 1)

    def compute(k):
        start, size = CHUNKS[k]
        mine = bufs[k][0]
        for n in range(GROUPS):
            block = g[start : start + size, n * 256 : (n + 1) * 256]
            cross = lax.dot_general(wt[n], block, nt, preferred_element_type=f32).astype(bf16)
            for h in range(2):
                ct[h, n * 128 : (n + 1) * 128, :size] = cross[h * 128 : (h + 1) * 128]
        for h in range(2):
            lags = jnp.dot(kt[...], ct[h, :, :size], preferred_element_type=f32) * SCALE
            for b4 in range(4):
                mine[b4 % 2, 2 * h + b4 // 2] = lags[b4 * PART : (b4 + 1) * PART].astype(bf16)

    sums = {}

    def send(name, n, k, src, dst, to):
        copy = pltpu.make_async_remote_copy(
            src_ref=src,
            dst_ref=dst,
            send_sem=r_send.at[k * 5 + n],
            recv_sem=r_recv.at[k * 5 + n],
            device_id=at_band(to),
            device_id_type=MESH,
        )
        copy.start()
        sums[(name, k)] = copy

    up, down, far = lax.rem(zh + 1, 4), lax.rem(zh + 3, 4), lax.rem(zh + 2, 4)
    to_sibling, to_up, to_down = 2 * zh + 1 - core, 2 * up + core, 2 * down + core

    def r0(k):
        compute(k)
        send("sib", 0, k, bufs[k][0].at[1 - core], bufs[k][1], to_sibling)

    def r1(k):
        mine, theirs, both, h1, h2, _ = bufs[k]
        sums[("sib", k)].wait_recv()
        for n in (far, up, down, zh):
            both[n] = (mine[core, n].astype(f32) + theirs[n].astype(f32)).astype(bf16)
            if n is far:
                send("ha", 1, k, both.at[far, pl.ds(0, HALF_A)], h1, to_up)
                send("hb", 2, k, both.at[far, pl.ds(HALF_A, PART - HALF_A)], h2, to_down)

    def r2(k):
        _, _, both, h1, h2, final = bufs[k]
        sums[("ha", k)].wait_recv()
        both[up, :HALF_A] = (both[up, :HALF_A].astype(f32) + h1[...].astype(f32)).astype(bf16)
        send("fu", 3, k, both.at[up], final.at[0], to_up)
        sums[("hb", k)].wait_recv()
        both[down, HALF_A:] = (both[down, HALF_A:].astype(f32) + h2[...].astype(f32)).astype(bf16)
        send("fd", 4, k, both.at[down], final.at[1], to_down)

    def r3(k):
        _, _, both, _, _, final = bufs[k]
        start, size = CHUNKS[k]
        sums[("fu", k)].wait_recv()
        sums[("fd", k)].wait_recv()
        whole = both[zh].astype(f32) + final[0].astype(f32) + final[1].astype(f32)
        out[:, start : start + size] = whole.astype(bf16)

    kt_copy.wait()
    arrive("fa", 1, 4)
    arrive("ba", 1, 3)
    r0(0)
    arrive("fb", 1, 3)
    arrive("bb", 1, 4)
    r1(0)
    arrive("fa", 2, 4)
    arrive("ba", 2, 3)
    r0(1)
    r2(0)
    arrive("fb", 2, 3)
    arrive("bb", 2, 4)
    r1(1)
    arrive("fa", 3, 4)
    arrive("ba", 3, 3)
    r0(2)
    r2(1)
    r3(0)
    arrive("fb", 3, 3)
    arrive("bb", 3, 4)
    r1(2)
    arrive("fa", 4, 4)
    arrive("bb", 4, 4)
    r0(3)
    r2(2)
    r1(3)
    r0(4)
    r3(1)
    r2(3)
    r1(4)
    r3(2)
    r2(4)
    r3(3)
    r3(4)

    for copy in exchange:
        copy.wait_send()
    for copy in copies.values():
        copy.wait_send()
    for copy in sums.values():
        copy.wait_send()


def _place_kernel(table, place, summed, select, out, turned):
    tile = lax.axis_index("tile")
    rows = lax.dot_general(
        summed[...], select[...], (((0,), (0,)), ((), ())), preferred_element_type=jnp.float32
    )
    turned[...] = rows.astype(jnp.bfloat16).reshape(turned.shape)

    def step(s, carry):
        partner = table[0, s]
        behind = lax.rem(tile // 2 - partner // 2 + TILE // 2, TILE // 2)
        block = place[behind] * 2 + lax.rem(partner, 2)
        for i4 in range(4):
            out[s, i4] = turned[block, :, i4 * 128 : i4 * 128 + LAGS]
        return carry

    lax.fori_loop(0, out.shape[0], step, 0)


def body(waveforms, band_widths, pair_table):
    slots = pair_table.shape[1]
    wave = jnp.transpose(waveforms, (1, 0, 2)).reshape(SEGL * CH, SAMPLES)
    wave = jnp.pad(wave, ((0, 0), (0, 512 - SAMPLES)))
    bf16 = jnp.bfloat16
    scratch = [
        pltpu.VMEM((BAND, 64, 128), bf16),
        pltpu.VMEM((BAND, 64, 128), bf16),
        pltpu.VMEM((JALL, WIDE), bf16),
        pltpu.VMEM((GROUPS, 256, 256), bf16),
        pltpu.VMEM((4 * PART, GROUPS * 128), bf16),
        pltpu.VMEM((2, GROUPS * 128, 256), bf16),
    ]
    for _, size in CHUNKS:
        scratch += [
            pltpu.VMEM((2, 4, PART, size), bf16),
            pltpu.VMEM((4, PART, size), bf16),
            pltpu.VMEM((4, PART, size), bf16),
            pltpu.VMEM((HALF_A, size), bf16),
            pltpu.VMEM((PART - HALF_A, size), bf16),
            pltpu.VMEM((2, PART, size), bf16),
        ]
    dma = pltpu.SemaphoreType.DMA
    scratch += [
        dma,
        dma((BAND,)),
        dma((BAND,)),
        dma((19,)),
        dma((19,)),
        dma((5 * len(CHUNKS),)),
        dma((5 * len(CHUNKS),)),
    ]
    vmem = pl.BlockSpec(memory_space=pltpu.VMEM)
    smem = pl.BlockSpec(memory_space=pltpu.SMEM)
    summed = pl.pallas_call(
        _main_kernel,
        out_shape=jax.ShapeDtypeStruct((PART, JALL), bf16),
        in_specs=[smem, vmem, vmem, pl.BlockSpec(memory_space=pl.ANY)],
        out_specs=vmem,
        scratch_shapes=scratch,
        compiler_params=pltpu.CompilerParams(
            collective_id=0, has_side_effects=True, vmem_limit_bytes=40 * 1024 * 1024
        ),
        name="correlate",
    )(band_widths, wave, jnp.asarray(_forward_const()), jnp.asarray(_inverse_const()))
    place = np.zeros((TILE // 2,), np.int32)
    for r, i in POS.items():
        place[r] = i
    placed = pl.pallas_call(
        _place_kernel,
        out_shape=jax.ShapeDtypeStruct((slots, 4, CH, LAGS), bf16),
        in_specs=[smem, smem, vmem, vmem],
        out_specs=vmem,
        scratch_shapes=[pltpu.VMEM((JALL // CH, CH, 512), bf16)],
        compiler_params=pltpu.CompilerParams(vmem_limit_bytes=32 * 1024 * 1024),
        name="place",
    )(pair_table, jnp.asarray(place), summed, jnp.asarray(_select_const()))
    return placed[None]


def solution(mesh):
    placed = (P("tile", "band", None), P(), P("tile", None))
    return jax.shard_map(
        body,
        mesh=mesh,
        in_specs=placed,
        out_specs=P("tile", None, "band", None, None),
        check_vma=False,
    )
```

```python
import functools
import math

import jax
import jax.numpy as jnp
import ml_dtypes
import numpy as np
from jax import lax
from jax.experimental import pallas as pl
from jax.experimental.pallas import tpu as pltpu
from jax.sharding import PartitionSpec as P

BINS = 180
FIRST = 20
LAGS = 51
SAMPLES = 500
EPS = 1e-05

BAND = 8
TILE = 64
CH = 32
SEG = 32
SEGL = 4
QN = 24
GROUPS = QN // 4
ROWS = 2 * QN
WIDE = QN * 64
PART = 208
HALF_A = 112
SCALE = 1.0 / math.sqrt(SEG * BINS)
MESH = pl.DeviceIdType.MESH

ORDER = [0, 8, 16, 1, 7, 9, 15, 2, 6, 10, 14, 3, 5, 11, 13, 4, 12]
POS = {r: i for i, r in enumerate(ORDER)}
CHUNKS = 9
JALL = 128 * CHUNKS


def _forward_const():
    n = np.arange(SAMPLES)
    table = np.zeros((BAND * QN, 2, SAMPLES), np.float32)
    for k in range(BINS):
        angle = ((n * (FIRST + k)) % SAMPLES) * (2.0 * math.pi / SAMPLES)
        table[k, 0] = np.cos(angle)
        table[k, 1] = -np.sin(angle)
    return table.reshape(BAND * ROWS, SAMPLES).astype(ml_dtypes.bfloat16)


def _inverse_const():
    tau = np.arange(LAGS) - LAGS // 2
    table = np.zeros((BAND * QN, 2, LAGS), np.float32)
    for k in range(BINS):
        angle = (((FIRST + k) * tau) % SAMPLES) * (2.0 * math.pi / SAMPLES)
        table[k, 0] = np.cos(angle)
        table[k, 1] = -np.sin(angle)
    table = table.reshape(BAND, GROUPS, 4, 2, LAGS)
    out = np.zeros((BAND, 4, PART, GROUPS, 4, 2, 16), np.float32)
    for b4 in range(4):
        for i4 in range(4):
            rows = np.moveaxis(table, -1, 1)
            out[:, b4, i4 * LAGS : (i4 + 1) * LAGS, :, :, :, b4 * 4 + i4] = rows
    return out.reshape(BAND, 4 * PART, GROUPS * 128).astype(ml_dtypes.bfloat16)


def _select_const():
    out = np.zeros((PART, 512), np.float32)
    for i4 in range(4):
        for lag in range(LAGS):
            out[i4 * LAGS + lag, i4 * 128 + lag] = 1.0
    return out.astype(ml_dtypes.bfloat16)


def _main_kernel(widths_hbm, wave_hbm, fwd_hbm, inv_all, out, *scratch):
    widths, wave, fwd, sb, rb, g, wt, kt, ct, parts, theirs, sums, h1, h2, final = scratch[:15]
    (in_sem, a_send, a_recv, g_send, g_recv, r_send, r_recv) = scratch[15:]
    f32, bf16 = jnp.float32, jnp.bfloat16

    band = lax.axis_index("band")
    tile = lax.axis_index("tile")
    core = lax.rem(band, 2)
    zh = band // 2
    z = lax.rem(tile, 2)
    y = lax.rem(tile // 2, 8)
    first = (7 - y) // 7
    last = (y + 1) // 8

    def at_band(b):
        return {"band": b, "tile": tile}

    def at_tile(t):
        return {"band": band, "tile": lax.rem(t + TILE, TILE)}

    barrier = pltpu.get_barrier_semaphore()
    peers = [at_band(lax.rem(band + o, BAND)) for o in range(1, BAND)]
    other_z = tile + 1 - 2 * z
    above, below = tile + 2 - 16 * last, tile - 2 + 16 * first
    peers += [at_tile(t) for t in (other_z, tile + 16, tile - 16, tile + 32)]
    peers += [at_tile(t) for t in (tile + 2, tile - 2, above, below)]
    for peer in peers:
        pl.semaphore_signal(barrier, inc=1, device_id=peer, device_id_type=MESH)
    wave_copy = pltpu.make_async_copy(wave_hbm, wave, in_sem.at[0])
    fwd_copy = pltpu.make_async_copy(fwd_hbm, fwd, in_sem.at[1])
    widths_copy = pltpu.make_async_copy(widths_hbm, widths, in_sem.at[2])
    kt_copy = pltpu.make_async_copy(inv_all.at[band], kt, in_sem.at[3])
    for copy in (wave_copy, fwd_copy, widths_copy, kt_copy):
        copy.start()
    g[1088:, :] = jnp.zeros((JALL - 1088, WIDE), bf16)
    wave_copy.wait()
    fwd_copy.wait()
    widths_copy.wait()

    nt = (((1,), (1,)), ((), ()))
    samples = jnp.concatenate([wave[:, s, :] for s in range(SEGL)], axis=0)
    spectra = lax.dot_general(fwd[...], samples, nt, preferred_element_type=f32).astype(bf16)
    values = spectra.astype(f32)
    squares = values * values
    sq_hi = squares.astype(bf16)
    sq_lo = (squares - sq_hi.astype(f32)).astype(bf16)
    offsets = []
    total = widths[0] * 0
    for b in range(BAND):
        offsets.append(total)
        total = total + widths[b]

    def member(rows, bins):
        low = jnp.zeros(rows.shape, jnp.int32)
        size = jnp.zeros(rows.shape, jnp.int32)
        for b in range(BAND):
            low = jnp.where(rows == b, offsets[b], low)
            size = jnp.where(rows == b, widths[b], size)
        return jnp.where((bins >= low) & (bins < low + size), 1.0, 0.0).astype(f32)

    shape = (BAND, BAND * ROWS)
    is_in = member(
        lax.broadcasted_iota(jnp.int32, shape, 0), lax.broadcasted_iota(jnp.int32, shape, 1) // 2
    ).astype(bf16)
    part = jnp.dot(is_in, sq_hi, preferred_element_type=f32)
    part = part + jnp.dot(is_in, sq_lo, preferred_element_type=f32)
    part_hi = part.astype(bf16).astype(f32)
    energies = jnp.concatenate([part_hi, part - part_hi], axis=0).astype(bf16)
    for b in range(BAND):
        sb[b, :ROWS] = spectra[b * ROWS : (b + 1) * ROWS]
        sb[b, ROWS:] = energies
    rb[0] = sb[band]

    pl.semaphore_wait(barrier, len(peers))

    exchange = []
    for o in range(1, BAND):
        to = lax.rem(band + o, BAND)
        copy = pltpu.make_async_remote_copy(
            src_ref=sb.at[to],
            dst_ref=rb.at[o],
            send_sem=a_send.at[o],
            recv_sem=a_recv.at[o],
            device_id=at_band(to),
            device_id_type=MESH,
        )
        copy.start()
        exchange.append(copy)
    for copy in exchange:
        copy.wait_recv()

    energy = jnp.zeros((BAND, 128), f32)
    for o in range(BAND):
        tail = rb[o, ROWS:].astype(f32)
        energy = energy + tail[:BAND] + tail[BAND:]
    energy = energy + pltpu.roll(energy, 64, 1)
    energy = energy + pltpu.roll(energy, 32, 1)
    row8 = lax.broadcasted_iota(jnp.int32, (BAND, 128), 0)
    width8 = jnp.ones((BAND, 128), f32)
    for b in range(BAND):
        width8 = jnp.where(row8 == b, widths[b].astype(f32), width8)
    gain = lax.rsqrt(energy / (SEG * width8) + EPS)
    bins = band * QN + lax.broadcasted_iota(jnp.int32, (ROWS, 128), 0) // 2
    gains = jnp.zeros((ROWS, 128), f32)
    for b in range(BAND):
        inside = (bins >= offsets[b]) & (bins < offsets[b] + widths[b])
        gains = jnp.where(inside, gain[b : b + 1, :], gains)
    white = [(rb[o, :ROWS].astype(f32) * gains).astype(bf16).astype(f32) for o in range(BAND)]

    lane = lax.broadcasted_iota(jnp.int32, (CH, 128), 1)
    own_row = pl.multiple_of(z * CH, CH)
    tiles = []
    for pair in range(GROUPS // 2):
        stack = jnp.concatenate(
            [white[o][(2 * pair + h) * 8 : (2 * pair + h + 1) * 8] for h in range(2) for o in range(BAND)],
            axis=0,
        )
        flipped = jnp.transpose(stack)
        rolled = pltpu.roll(flipped, 64, 1)
        seg = [flipped[s * CH : (s + 1) * CH] for s in range(SEGL)]
        seg_r = [rolled[s * CH : (s + 1) * CH] for s in range(SEGL)]
        for h in range(2):
            low, high = (seg, seg_r) if h == 0 else (seg_r, seg)
            halves = [jnp.where(lane < 64, low[2 * v], high[2 * v + 1]) for v in range(2)]
            tiles.append(halves)
            base = (2 * pair + h) * 256
            for v in range(2):
                g[pl.ds(own_row, CH), base + v * 128 : base + (v + 1) * 128] = halves[v].astype(bf16)

    def slot(r, half=None, instead=None, when=None):
        row = POS[r] * 64
        if half is not None:
            return g.at[pl.ds(pl.multiple_of(row + half * CH, CH), CH)]
        if instead is not None:
            row = pl.multiple_of(row + when * (POS[instead] - POS[r]) * 64, 64)
        return g.at[pl.ds(row, 64)]

    copies = {}

    def describe(name, src, dst, to):
        n = len(copies)
        copies[name] = pltpu.make_async_remote_copy(
            src_ref=src,
            dst_ref=dst,
            send_sem=g_send.at[n],
            recv_sem=g_recv.at[n],
            device_id=at_tile(to),
            device_id_type=MESH,
        )

    describe("z", slot(0, z), slot(0, z), other_z)
    for name, half in (("", z), ("s", 1 - z)):
        describe("x1" + name, slot(0, half), slot(8, half), tile + 16)
        describe("x2" + name, slot(0, half), slot(16, half), tile + 32)
    for k in range(1, 5):
        describe(k, slot(k - 1, instead=7 + k, when=last), slot(k), above)
        if k < 4:
            describe(8 - k, slot(9 - k), slot(8 - k), tile - 2)
        if 1 < k < 4:
            describe(8 + k, slot(7 + k), slot(8 + k), tile + 2)
        if k > 1:
            describe(16 - k, slot(17 - k, instead=9 - k, when=first), slot(16 - k), below)
    describe(9, slot(1), slot(9), tile + 16)
    describe(15, slot(7), slot(15), tile + 16)

    def start(name):
        copies[name].start()

    def arrive(r):
        if r == 0:
            copies["z"].wait_recv()
            start("x1s")
            start("x2s")
            pl.when(last == 0)(lambda: start(1))
        elif r in (8, 16):
            name = {8: "x1", 16: "x2"}[r]
            copies[name].wait_recv()
            copies[name + "s"].wait_recv()
            if r == 8:
                pl.when(last == 1)(lambda: start(1))
                start(7)
        else:
            copies[r].wait_recv()
            if r < 4:
                pl.when(last == 0)(lambda: start(r + 1))
                if r == 1:
                    start(9)
            elif 4 < r < 8:
                if r == 7:
                    start(15)
                if r > 5:
                    start(r - 1)
                pl.when(first == 1)(lambda: start(r + 7))
            elif 8 < r < 12:
                pl.when(last == 1)(lambda: start(r - 7))
                if r < 11:
                    start(r + 1)
            elif r > 12:
                pl.when(first == 0)(lambda: start(r - 1))

    start("z")
    start("x1")
    start("x2")

    even = lax.rem(lane, 2) == 0
    bin4 = lax.rem(lane // 2, 4)
    for n, halves in enumerate(tiles):
        for v in range(2):
            own = halves[v]
            alt = jnp.where(even, pltpu.roll(own, 127, 1), -pltpu.roll(own, 1, 1))
            for q in range(4):
                for p in range(2):
                    kept = jnp.where(bin4 == q, own if p == 0 else alt, 0.0).astype(bf16)
                    for h in range(2):
                        row = h * 128 + q * 32 + p * 16
                        wt[n, row : row + 16, v * 128 : (v + 1) * 128] = kept[h * 16 : h * 16 + 16]

    def compute(k):
        for n in range(GROUPS):
            block = g[k * 128 : (k + 1) * 128, n * 256 : (n + 1) * 256]
            cross = lax.dot_general(wt[n], block, nt, preferred_element_type=f32).astype(bf16)
            for h in range(2):
                ct[n * 128 : (n + 1) * 128, h * 128 : (h + 1) * 128] = cross[h * 128 : (h + 1) * 128]
        lags = jnp.dot(kt[...], ct[...], preferred_element_type=f32) * SCALE
        for h in range(2):
            for b4 in range(4):
                share = lags[b4 * PART : (b4 + 1) * PART, h * 128 : (h + 1) * 128]
                parts[k, b4 % 2, 2 * h + b4 // 2] = share.astype(bf16)

    adding = {}

    def send(name, n, k, src, dst, to):
        copy = pltpu.make_async_remote_copy(
            src_ref=src,
            dst_ref=dst,
            send_sem=r_send.at[k * 5 + n],
            recv_sem=r_recv.at[k * 5 + n],
            device_id=at_band(to),
            device_id_type=MESH,
        )
        copy.start()
        adding[(name, k)] = copy

    up, down, far = lax.rem(zh + 1, 4), lax.rem(zh + 3, 4), lax.rem(zh + 2, 4)
    to_sibling, to_up, to_down = 2 * zh + 1 - core, 2 * up + core, 2 * down + core

    def r0(k):
        compute(k)
        send("sib", 0, k, parts.at[k, 1 - core], theirs.at[k], to_sibling)

    def r1(k):
        adding[("sib", k)].wait_recv()
        for n in (far, up, down, zh):
            both = parts[k, core, n].astype(f32) + theirs[k, n].astype(f32)
            sums[k, n] = both.astype(bf16)
            if n is far:
                send("ha", 1, k, sums.at[k, far, pl.ds(0, HALF_A)], h1.at[k], to_up)
                send("hb", 2, k, sums.at[k, far, pl.ds(HALF_A, PART - HALF_A)], h2.at[k], to_down)

    def r2(k):
        adding[("ha", k)].wait_recv()
        both = sums[k, up, :HALF_A].astype(f32) + h1[k].astype(f32)
        sums[k, up, :HALF_A] = both.astype(bf16)
        send("fu", 3, k, sums.at[k, up], final.at[k, 0], to_up)
        adding[("hb", k)].wait_recv()
        both = sums[k, down, HALF_A:].astype(f32) + h2[k].astype(f32)
        sums[k, down, HALF_A:] = both.astype(bf16)
        send("fd", 4, k, sums.at[k, down], final.at[k, 1], to_down)

    def r3(k):
        adding[("fu", k)].wait_recv()
        adding[("fd", k)].wait_recv()
        whole = sums[k, zh].astype(f32) + final[k, 0].astype(f32) + final[k, 1].astype(f32)
        out[:, k * 128 : (k + 1) * 128] = whole.astype(bf16)

    kt_copy.wait()
    for k in range(CHUNKS):
        for r in ORDER[2 * k : 2 * k + 2]:
            arrive(r)
        r0(k)
        if k >= 2:
            r2(k - 2)
        if k >= 4:
            r3(k - 4)
        r1(k)
    r2(CHUNKS - 2)
    r2(CHUNKS - 1)
    for k in range(CHUNKS - 4, CHUNKS):
        r3(k)

    for copy in exchange:
        copy.wait_send()
    for copy in copies.values():
        copy.wait_send()
    for copy in adding.values():
        copy.wait_send()


def _place_kernel(table, place, summed, select, out, turned):
    tile = lax.axis_index("tile")
    rows = lax.dot_general(
        summed[...], select[...], (((0,), (0,)), ((), ())), preferred_element_type=jnp.float32
    )
    turned[...] = rows.astype(jnp.bfloat16).reshape(turned.shape)

    def step(s, carry):
        partner = table[0, s]
        behind = lax.rem(tile // 2 - partner // 2 + TILE // 2, TILE // 2)
        block = place[behind] * 2 + lax.rem(partner, 2)
        for i4 in range(4):
            out[s, i4] = turned[block, :, i4 * 128 : i4 * 128 + LAGS]
        return carry

    lax.fori_loop(0, out.shape[0], step, 0)


def body(waveforms, band_widths, pair_table):
    slots = pair_table.shape[1]
    bf16 = jnp.bfloat16
    scratch = [
        pltpu.SMEM((BAND,), jnp.int32),
        pltpu.VMEM(waveforms.shape, bf16),
        pltpu.VMEM((BAND * ROWS, SAMPLES), bf16),
        pltpu.VMEM((BAND, 64, 128), bf16),
        pltpu.VMEM((BAND, 64, 128), bf16),
        pltpu.VMEM((JALL, WIDE), bf16),
        pltpu.VMEM((GROUPS, 256, 256), bf16),
        pltpu.VMEM((4 * PART, GROUPS * 128), bf16),
        pltpu.VMEM((GROUPS * 128, 256), bf16),
        pltpu.VMEM((CHUNKS, 2, 4, PART, 128), bf16),
        pltpu.VMEM((CHUNKS, 4, PART, 128), bf16),
        pltpu.VMEM((CHUNKS, 4, PART, 128), bf16),
        pltpu.VMEM((CHUNKS, HALF_A, 128), bf16),
        pltpu.VMEM((CHUNKS, PART - HALF_A, 128), bf16),
        pltpu.VMEM((CHUNKS, 2, PART, 128), bf16),
    ]
    dma = pltpu.SemaphoreType.DMA
    scratch += [
        dma((4,)),
        dma((BAND,)),
        dma((BAND,)),
        dma((19,)),
        dma((19,)),
        dma((5 * CHUNKS,)),
        dma((5 * CHUNKS,)),
    ]
    vmem = pl.BlockSpec(memory_space=pltpu.VMEM)
    smem = pl.BlockSpec(memory_space=pltpu.SMEM)
    summed = pl.pallas_call(
        _main_kernel,
        out_shape=jax.ShapeDtypeStruct((PART, JALL), bf16),
        in_specs=[pl.BlockSpec(memory_space=pl.ANY)] * 4,
        out_specs=vmem,
        scratch_shapes=scratch,
        compiler_params=pltpu.CompilerParams(
            collective_id=0, has_side_effects=True, vmem_limit_bytes=60 * 1024 * 1024
        ),
        name="correlate",
    )(band_widths, waveforms, jnp.asarray(_forward_const()), jnp.asarray(_inverse_const()))
    place = np.zeros((TILE // 2,), np.int32)
    for r, i in POS.items():
        place[r] = i
    placed = pl.pallas_call(
        _place_kernel,
        out_shape=jax.ShapeDtypeStruct((slots, 4, CH, LAGS), bf16),
        in_specs=[smem, smem, vmem, vmem],
        out_specs=vmem,
        scratch_shapes=[pltpu.VMEM((JALL // CH, CH, 512), bf16)],
        compiler_params=pltpu.CompilerParams(vmem_limit_bytes=32 * 1024 * 1024),
        name="place",
    )(pair_table, jnp.asarray(place), summed, jnp.asarray(_select_const()))
    return placed[None]


def solution(mesh):
    placed = (P("tile", "band", None), P(), P("tile", None))
    return jax.shard_map(
        body,
        mesh=mesh,
        in_specs=placed,
        out_specs=P("tile", None, "band", None, None),
        check_vma=False,
    )
```

```python
import functools
import math

import jax
import jax.numpy as jnp
import ml_dtypes
import numpy as np
from jax import lax
from jax.experimental import pallas as pl
from jax.experimental.pallas import tpu as pltpu
from jax.sharding import PartitionSpec as P

BINS = 180
FIRST = 20
LAGS = 51
SAMPLES = 500
EPS = 1e-05

BAND = 8
TILE = 64
CH = 32
SEG = 32
SEGL = 4
QN = 48
BINGROUPS = 4
GROUPS = QN // 4
ROWS = 2 * QN
MSG = ROWS + 16
WIDE = QN * 64
PART = 208
SCALE = 1.0 / math.sqrt(SEG * BINS)
MESH = pl.DeviceIdType.MESH

ORDER = [0, 8, 16, 1, 7, 9, 15, 2, 6, 10, 14, 3, 5, 11, 13, 4, 12]
POS = {r: i for i, r in enumerate(ORDER)}
CHUNKS = [(0, 4), (4, 4), (8, 4), (12, 2), (14, 2), (16, 1)]
PACKED = {4: PART, 2: 112, 1: 64}
REGION = 640
JALL = 2 * REGION
STEPS = [
    "8a", "1a", "1b", "8b", "16b", "16a", "7a", "9a", "9b", "7b", "c0",
    "2a", "15a", "s0", "2b", "15b", "10a", "10b", "6a", "c1",
    "3a", "s1", "6b", "14a", "3b", "14b", "c2",
    "5a", "m0", "11b", "11a", "5b", "s2", "c3",
    "13a", "4a", "m1", "s3", "4b", "13b", "c4",
    "s4", "12a", "m2", "12b", "c5",
    "s5", "m3", "m4", "m5", "f0", "f1", "f2", "f3", "f4", "f5",
]


def _forward_const():
    n = np.arange(SAMPLES)
    table = np.zeros((BINGROUPS * QN, 2, SAMPLES), np.float32)
    for k in range(BINS):
        angle = ((n * (FIRST + k)) % SAMPLES) * (2.0 * math.pi / SAMPLES)
        table[k, 0] = np.cos(angle)
        table[k, 1] = -np.sin(angle)
    return table.reshape(BINGROUPS * ROWS, SAMPLES).astype(ml_dtypes.bfloat16)


def _inverse_const():
    tau = np.arange(LAGS) - LAGS // 2
    table = np.zeros((BINGROUPS * QN, 2, LAGS), np.float32)
    for k in range(BINS):
        angle = (((FIRST + k) * tau) % SAMPLES) * (2.0 * math.pi / SAMPLES)
        table[k, 0] = np.cos(angle)
        table[k, 1] = -np.sin(angle)
    table = table.reshape(BINGROUPS, GROUPS, 4, 2, LAGS)
    out = np.zeros((BINGROUPS, 4, PART, GROUPS, 4, 2, 16), np.float32)
    for b4 in range(4):
        for i4 in range(4):
            rows = np.moveaxis(table, -1, 1)
            out[:, b4, i4 * LAGS : (i4 + 1) * LAGS, :, :, :, b4 * 4 + i4] = rows
    return out.reshape(BINGROUPS, 4 * PART, GROUPS * 128).astype(ml_dtypes.bfloat16)


def _select_const():
    out = np.zeros((PART, 512), np.float32)
    for i4 in range(4):
        for lag in range(LAGS):
            out[i4 * LAGS + lag, i4 * 128 + lag] = 1.0
    return out.astype(ml_dtypes.bfloat16)


def _main_kernel(widths_hbm, wave_hbm, fwd_hbm, inv_all, out, *scratch):
    widths, wave, fwd, sb, rb, g, wt, kt, ct = scratch[:9]
    parts, theirs, mine, pair_out, pair_in, outer, final = scratch[9:16]
    (in_sem, a_send, a_recv, o_send, o_recv, g_send, g_recv, r_send, r_recv) = scratch[16:]
    f32, bf16 = jnp.float32, jnp.bfloat16

    band = lax.axis_index("band")
    tile = lax.axis_index("tile")
    core = lax.rem(band, 2)
    zh = band // 2
    z = lax.rem(tile, 2)
    side = band // 4
    group = lax.rem(band, BINGROUPS)
    home = z == side
    y = lax.rem(tile // 2, 8)
    first = (7 - y) // 7
    last = (y + 1) // 8

    def at_band(b):
        return {"band": b, "tile": tile}

    def at_tile(t):
        return {"band": band, "tile": lax.rem(t + TILE, TILE)}

    barrier = pltpu.get_barrier_semaphore()
    peers = [at_band(lax.rem(band + o, BAND)) for o in range(1, BAND)]
    other_z = tile + 1 - 2 * z
    above, below = tile + 2 - 16 * last, tile - 2 + 16 * first
    peers += [at_tile(t) for t in (tile + 16, tile - 16, tile + 32)]
    peers += [at_tile(t) for t in (tile + 2, tile - 2, above, below)]
    for peer in peers:
        pl.semaphore_signal(barrier, inc=1, device_id=peer, device_id_type=MESH)

    @pl.when(jnp.logical_not(home))
    def _():
        for b in range(BAND):
            peer = {"band": b, "tile": other_z}
            pl.semaphore_signal(barrier, inc=1, device_id=peer, device_id_type=MESH)

    wave_copy = pltpu.make_async_copy(wave_hbm, wave, in_sem.at[0])
    fwd_copy = pltpu.make_async_copy(fwd_hbm, fwd, in_sem.at[1])
    widths_copy = pltpu.make_async_copy(widths_hbm, widths, in_sem.at[2])
    kt_copy = pltpu.make_async_copy(inv_all.at[group], kt, in_sem.at[3])
    for copy in (wave_copy, fwd_copy, widths_copy, kt_copy):
        copy.start()
    wave_copy.wait()
    fwd_copy.wait()
    widths_copy.wait()

    nt = (((1,), (1,)), ((), ()))
    samples = jnp.concatenate([wave[:, s, :] for s in range(SEGL)], axis=0)
    spectra = lax.dot_general(fwd[...], samples, nt, preferred_element_type=f32).astype(bf16)
    values = spectra.astype(f32)
    squares = values * values
    sq_hi = squares.astype(bf16)
    sq_lo = (squares - sq_hi.astype(f32)).astype(bf16)
    offsets = []
    total = widths[0] * 0
    for b in range(BAND):
        offsets.append(total)
        total = total + widths[b]

    def member(rows, bins):
        low = jnp.zeros(rows.shape, jnp.int32)
        size = jnp.zeros(rows.shape, jnp.int32)
        for b in range(BAND):
            low = jnp.where(rows == b, offsets[b], low)
            size = jnp.where(rows == b, widths[b], size)
        return jnp.where((bins >= low) & (bins < low + size), 1.0, 0.0).astype(f32)

    shape = (BAND, BINGROUPS * ROWS)
    is_in = member(
        lax.broadcasted_iota(jnp.int32, shape, 0), lax.broadcasted_iota(jnp.int32, shape, 1) // 2
    ).astype(bf16)
    part = jnp.dot(is_in, sq_hi, preferred_element_type=f32)
    part = part + jnp.dot(is_in, sq_lo, preferred_element_type=f32)
    part_hi = part.astype(bf16).astype(f32)
    energies = jnp.concatenate([part_hi, part - part_hi], axis=0).astype(bf16)
    for b in range(BINGROUPS):
        sb[b, :ROWS] = spectra[b * ROWS : (b + 1) * ROWS]
        sb[b, ROWS:] = energies
    rb[0, 0] = sb[group]

    pl.semaphore_wait(barrier, len(peers) + BINGROUPS)

    exchange = []
    for o in range(1, BAND):
        to = lax.rem(band + o, BAND)
        copy = pltpu.make_async_remote_copy(
            src_ref=sb.at[lax.rem(to, BINGROUPS)],
            dst_ref=rb.at[0, o],
            send_sem=a_send.at[o],
            recv_sem=a_recv.at[o],
            device_id=at_band(to),
            device_id_type=MESH,
        )
        copy.start()
        exchange.append(copy)
    across = []
    for j in range(BINGROUPS):
        to = 4 * z + j
        o = lax.rem(to - band + BAND, BAND)
        copy = pltpu.make_async_remote_copy(
            src_ref=sb.at[j],
            dst_ref=rb.at[1, o],
            send_sem=o_send.at[j],
            recv_sem=o_recv.at[o],
            device_id={"band": to, "tile": other_z},
            device_id_type=MESH,
        )
        copy.start()
        across.append(copy)

    lane = lax.broadcasted_iota(jnp.int32, (CH, 128), 1)

    def whiten(which):
        energy = jnp.zeros((BAND, 128), f32)
        for o in range(BAND):
            tail = rb[which, o, ROWS:].astype(f32)
            energy = energy + tail[:BAND] + tail[BAND:]
        energy = energy + pltpu.roll(energy, 64, 1)
        energy = energy + pltpu.roll(energy, 32, 1)
        row8 = lax.broadcasted_iota(jnp.int32, (BAND, 128), 0)
        width8 = jnp.ones((BAND, 128), f32)
        for b in range(BAND):
            width8 = jnp.where(row8 == b, widths[b].astype(f32), width8)
        gain = lax.rsqrt(energy / (SEG * width8) + EPS)
        bins = group * QN + lax.broadcasted_iota(jnp.int32, (ROWS, 128), 0) // 2
        gains = jnp.zeros((ROWS, 128), f32)
        for b in range(BAND):
            inside = (bins >= offsets[b]) & (bins < offsets[b] + widths[b])
            gains = jnp.where(inside, gain[b : b + 1, :], gains)
        white = [
            (rb[which, o, :ROWS].astype(f32) * gains).astype(bf16).astype(f32) for o in range(BAND)
        ]
        tiles = []
        for pair in range(GROUPS // 2):
            stack = jnp.concatenate(
                [
                    white[o][(2 * pair + h) * 8 : (2 * pair + h + 1) * 8]
                    for h in range(2)
                    for o in range(BAND)
                ],
                axis=0,
            )
            flipped = jnp.transpose(stack)
            rolled = pltpu.roll(flipped, 64, 1)
            seg = [flipped[s * CH : (s + 1) * CH] for s in range(SEGL)]
            seg_r = [rolled[s * CH : (s + 1) * CH] for s in range(SEGL)]
            for low, high in ((seg, seg_r), (seg_r, seg)):
                tiles.append([jnp.where(lane < 64, low[2 * v], high[2 * v + 1]) for v in range(2)])
        return tiles

    for copy in exchange:
        copy.wait_recv()

    @pl.when(jnp.logical_not(home))
    def _():
        for o in range(BAND):
            pltpu.make_async_remote_copy(
                src_ref=sb.at[0],
                dst_ref=rb.at[1, o],
                send_sem=o_send.at[0],
                recv_sem=o_recv.at[o],
                device_id={"band": band, "tile": other_z},
                device_id_type=MESH,
            ).wait_recv()

    for n, halves in enumerate(whiten(lax.rem(z + side, 2))):
        for v in range(2):
            g[:CH, n * 256 + v * 128 : n * 256 + (v + 1) * 128] = halves[v].astype(bf16)

    def slot(r, h, instead=None, when=None):
        row = POS[r] * CH
        if instead is not None:
            row = pl.multiple_of(row + when * (POS[instead] - POS[r]) * CH, CH)
        return g.at[pl.ds(row, CH), pl.ds(h * (WIDE // 2), WIDE // 2)]

    copies = {}

    def describe(name, src, dst, to):
        n = len(copies)
        copies[name] = pltpu.make_async_remote_copy(
            src_ref=src,
            dst_ref=dst,
            send_sem=g_send.at[n],
            recv_sem=g_recv.at[n],
            device_id=at_tile(to),
            device_id_type=MESH,
        )

    for h in range(2):
        describe((8, h), slot(0, h), slot(8, h), tile + 16)
        describe((16, h), slot(0, h), slot(16, h), tile + 32)
        for k in range(1, 5):
            describe((k, h), slot(k - 1, h, 7 + k, last), slot(k, h), above)
            if k < 4:
                describe((8 - k, h), slot(9 - k, h), slot(8 - k, h), tile - 2)
            if 1 < k < 4:
                describe((8 + k, h), slot(7 + k, h), slot(8 + k, h), tile + 2)
            if k > 1:
                describe((16 - k, h), slot(17 - k, h, 9 - k, first), slot(16 - k, h), below)
        describe((9, h), slot(1, h), slot(9, h), tile + 16)
        describe((15, h), slot(7, h), slot(15, h), tile + 16)

    def arrive(r, h):
        def start(other):
            copies[(other, h)].start()

        if r:
            copies[(r, h)].wait_recv()
        if r == 0:
            pl.when(last == 0)(lambda: start(1))
            start(8)
            start(16)
        elif r == 8:
            pl.when(last == 1)(lambda: start(1))
            start(7)
        elif r < 4:
            pl.when(last == 0)(lambda: start(r + 1))
            if r == 1:
                start(9)
        elif 4 < r < 8:
            if r > 5:
                start(r - 1)
            pl.when(first == 1)(lambda: start(r + 7))
            if r == 7:
                start(15)
        elif 8 < r < 12:
            pl.when(last == 1)(lambda: start(r - 7))
            if r < 11:
                start(r + 1)
        elif 12 < r < 16:
            pl.when(first == 0)(lambda: start(r - 1))

    arrive(0, 0)
    arrive(0, 1)

    even = lax.rem(lane, 2) == 0
    bin4 = lax.rem(lane // 2, 4)
    for n, halves in enumerate(whiten(0)):
        for v in range(2):
            own = halves[v]
            alt = jnp.where(even, pltpu.roll(own, 127, 1), -pltpu.roll(own, 1, 1))
            for q in range(4):
                for p in range(2):
                    kept = jnp.where(bin4 == q, own if p == 0 else alt, 0.0).astype(bf16)
                    for h in range(2):
                        row = h * 128 + q * 32 + p * 16
                        wt[n, row : row + 16, v * 128 : (v + 1) * 128] = kept[h * 16 : h * 16 + 16]

    wide = lax.broadcasted_iota(jnp.int32, (PART, 128), 1)

    def compute(k):
        start, blocks = CHUNKS[k]
        rows = PACKED[blocks]
        for n in range(GROUPS):
            block = g[start * CH : (start + blocks) * CH, n * 256 : (n + 1) * 256]
            block = jnp.concatenate([block] * (4 // blocks), axis=0)
            cross = lax.dot_general(wt[n], block, nt, preferred_element_type=f32).astype(bf16)
            for h in range(2):
                ct[n * 128 : (n + 1) * 128, h * 128 : (h + 1) * 128] = cross[h * 128 : (h + 1) * 128]
        lags = jnp.dot(kt[...], ct[...], preferred_element_type=f32) * SCALE
        for h in range(2):
            for b4 in range(4):
                share = lags[b4 * PART : (b4 + 1) * PART, h * 128 : (h + 1) * 128]
                if blocks < 4:
                    copies_of = 4 // blocks
                    step = (PART - rows) // (copies_of - 1)
                    packed = share[:rows]
                    for i in range(1, copies_of):
                        here = wide[:rows] // (32 * blocks) == i
                        packed = jnp.where(here, share[i * step : i * step + rows], packed)
                    share = packed
                parts[k, b4 % 2, 2 * h + b4 // 2, :rows] = share.astype(bf16)

    def place(k, region, share):
        start, blocks = CHUNKS[k]
        rows = PACKED[blocks]
        base = region * REGION + start * CH
        if blocks < 4:
            copies_of = 4 // blocks
            step = (PART - rows) // (copies_of - 1)
            pieces = [share]
            for i in range(1, copies_of):
                pieces.append(pltpu.roll(share, 128 - 32 * blocks * i, 1)[rows - step :])
            share = jnp.concatenate(pieces, axis=0)
            shift = base % 128
            if shift:
                share = pltpu.roll(share, shift, 1)
            out[:, base : base + 32 * blocks] = share[:, shift : shift + 32 * blocks].astype(bf16)
        else:
            out[:, base : base + 128] = share.astype(bf16)

    adding = {}

    def send(name, n, k, src, dst, to):
        copy = pltpu.make_async_remote_copy(
            src_ref=src,
            dst_ref=dst,
            send_sem=r_send.at[k * 3 + n],
            recv_sem=r_recv.at[k * 3 + n],
            device_id=at_band(to),
            device_id_type=MESH,
        )
        copy.start()
        adding[(name, k)] = copy

    odd = lax.rem(zh, 2)
    mate, beyond, far = zh + 1 - 2 * odd, lax.rem(zh + 2 * odd + 3, 4), lax.rem(zh + 2, 4)
    to_sibling, to_mate, to_beyond = 2 * zh + 1 - core, 2 * mate + core, 2 * beyond + core

    def r0(k):
        compute(k)
        rows = pl.ds(0, PACKED[CHUNKS[k][1]])
        send("sib", 0, k, parts.at[k, 1 - core, :, rows], theirs.at[k, :, rows], to_sibling)

    def r1(k):
        rows = PACKED[CHUNKS[k][1]]
        adding[("sib", k)].wait_recv()

        def both(n):
            return parts[k, core, n, :rows].astype(f32) + theirs[k, n, :rows].astype(f32)

        pair_out[k, 0, :rows] = both(mate).astype(bf16)
        pair_out[k, 1, :rows] = both(far).astype(bf16)
        cut = pl.ds(0, rows)
        send("pair", 1, k, pair_out.at[k, :, cut], pair_in.at[k, :, cut], to_mate)
        outer[k, :rows] = both(beyond).astype(bf16)
        mine[k, :rows] = both(zh).astype(bf16)

    def r2(k):
        rows = PACKED[CHUNKS[k][1]]
        adding[("pair", k)].wait_recv()
        outer[k, :rows] = (outer[k, :rows].astype(f32) + pair_in[k, 1, :rows].astype(f32)).astype(bf16)
        send("out", 2, k, outer.at[k, pl.ds(0, rows)], final.at[k, pl.ds(0, rows)], to_beyond)
        place(k, 0, mine[k, :rows].astype(f32) + pair_in[k, 0, :rows].astype(f32))

    def r3(k):
        rows = PACKED[CHUNKS[k][1]]
        adding[("out", k)].wait_recv()
        place(k, 1, final[k, :rows].astype(f32))

    kt_copy.wait()
    out[:, 17 * CH : REGION] = jnp.zeros((PART, REGION - 17 * CH), bf16)
    out[:, REGION + 17 * CH :] = jnp.zeros((PART, REGION - 17 * CH), bf16)
    stages = {"c": r0, "s": r1, "m": r2, "f": r3}
    for step in STEPS:
        if step[0] in stages:
            stages[step[0]](int(step[1:]))
        else:
            arrive(int(step[:-1]), "ab".index(step[-1]))

    for copy in exchange + across:
        copy.wait_send()
    for copy in copies.values():
        copy.wait_send()
    for copy in adding.values():
        copy.wait_send()


def _place_kernel(table, place, summed, select, out, turned):
    tile = lax.axis_index("tile")
    side = lax.axis_index("band") // 4
    rows = lax.dot_general(
        summed[...], select[...], (((0,), (0,)), ((), ())), preferred_element_type=jnp.float32
    )
    turned[...] = rows.astype(jnp.bfloat16).reshape(turned.shape)

    def step(s, carry):
        partner = table[0, s]
        behind = lax.rem(tile // 2 - partner // 2 + TILE // 2, TILE // 2)
        other = lax.rem(partner + side, 2)
        block = place[behind] + other * (REGION // CH)
        for i4 in range(4):
            out[s, i4] = turned[block, :, i4 * 128 : i4 * 128 + LAGS]
        return carry

    lax.fori_loop(0, out.shape[0], step, 0)


def body(waveforms, band_widths, pair_table):
    slots = pair_table.shape[1]
    bf16 = jnp.bfloat16
    scratch = [
        pltpu.SMEM((BAND,), jnp.int32),
        pltpu.VMEM(waveforms.shape, bf16),
        pltpu.VMEM((BINGROUPS * ROWS, SAMPLES), bf16),
        pltpu.VMEM((BINGROUPS, MSG, 128), bf16),
        pltpu.VMEM((2, BAND, MSG, 128), bf16),
        pltpu.VMEM((17 * CH, WIDE), bf16),
        pltpu.VMEM((GROUPS, 256, 256), bf16),
        pltpu.VMEM((4 * PART, GROUPS * 128), bf16),
        pltpu.VMEM((GROUPS * 128, 256), bf16),
        pltpu.VMEM((len(CHUNKS), 2, 4, PART, 128), bf16),
        pltpu.VMEM((len(CHUNKS), 4, PART, 128), bf16),
        pltpu.VMEM((len(CHUNKS), PART, 128), bf16),
        pltpu.VMEM((len(CHUNKS), 2, PART, 128), bf16),
        pltpu.VMEM((len(CHUNKS), 2, PART, 128), bf16),
        pltpu.VMEM((len(CHUNKS), PART, 128), bf16),
        pltpu.VMEM((len(CHUNKS), PART, 128), bf16),
    ]
    dma = pltpu.SemaphoreType.DMA
    scratch += [
        dma((4,)),
        dma((BAND,)),
        dma((BAND,)),
        dma((BINGROUPS,)),
        dma((BAND,)),
        dma((32,)),
        dma((32,)),
        dma((3 * len(CHUNKS),)),
        dma((3 * len(CHUNKS),)),
    ]
    vmem = pl.BlockSpec(memory_space=pltpu.VMEM)
    smem = pl.BlockSpec(memory_space=pltpu.SMEM)
    summed = pl.pallas_call(
        _main_kernel,
        out_shape=jax.ShapeDtypeStruct((PART, JALL), bf16),
        in_specs=[pl.BlockSpec(memory_space=pl.ANY)] * 4,
        out_specs=vmem,
        scratch_shapes=scratch,
        compiler_params=pltpu.CompilerParams(
            collective_id=0, has_side_effects=True, vmem_limit_bytes=60 * 1024 * 1024
        ),
        name="correlate",
    )(band_widths, waveforms, jnp.asarray(_forward_const()), jnp.asarray(_inverse_const()))
    place = np.zeros((TILE // 2,), np.int32)
    for r, i in POS.items():
        place[r] = i
    placed = pl.pallas_call(
        _place_kernel,
        out_shape=jax.ShapeDtypeStruct((slots, 4, CH, LAGS), bf16),
        in_specs=[smem, smem, vmem, vmem],
        out_specs=vmem,
        scratch_shapes=[pltpu.VMEM((JALL // CH, CH, 512), bf16)],
        compiler_params=pltpu.CompilerParams(vmem_limit_bytes=32 * 1024 * 1024),
        name="place",
    )(pair_table, jnp.asarray(place), summed, jnp.asarray(_select_const()))
    return placed[None]


def solution(mesh):
    placed = (P("tile", "band", None), P(), P("tile", None))
    return jax.shard_map(
        body,
        mesh=mesh,
        in_specs=placed,
        out_specs=P("tile", None, "band", None, None),
        check_vma=False,
    )
```

```python
import functools
import math

import jax
import jax.numpy as jnp
import ml_dtypes
import numpy as np
from jax import lax
from jax.experimental import pallas as pl
from jax.experimental.pallas import tpu as pltpu
from jax.sharding import PartitionSpec as P

BINS = 180
FIRST = 20
LAGS = 51
SAMPLES = 500
EPS = 1e-05

BAND = 8
TILE = 64
CH = 32
SEG = 32
SEGL = 4
QN = 48
BINGROUPS = 4
GROUPS = QN // 4
ROWS = 2 * QN
MSG = ROWS + 16
WIDE = QN * 64
PART = 208
SCALE = 1.0 / math.sqrt(SEG * BINS)
MESH = pl.DeviceIdType.MESH

ORDER = [0, 8, 16, 1, 7, 9, 15, 2, 6, 10, 14, 3, 5, 11, 13, 4, 12]
POS = {r: i for i, r in enumerate(ORDER)}
CHUNKS = [(0, 4), (4, 4), (8, 4), (12, 2), (14, 2), (16, 1)]
PACKED = {4: PART, 2: 112, 1: 64}
DIRECT = (4, 5)
STEPS = [
    "1b", "7a", "9a", "16a", "16b", "7b", "9b", "c0",
    "2a", "15a", "s0", "2b", "15b", "10a", "10b", "6a", "c1",
    "3a", "s1", "6b", "14a", "3b", "14b", "c2",
    "5a", "m0", "11b", "11a", "5b", "s2", "c3",
    "13a", "4a", "m1", "s3", "4b", "13b", "c4",
    "s4", "12a", "m2", "12b", "c5",
    "m3", "s5", "f0", "f1", "f2", "f3", "m4", "f4", "m5", "f5",
]


def _forward_const():
    n = np.arange(SAMPLES)
    table = np.zeros((BINGROUPS * QN, 2, SAMPLES), np.float32)
    for k in range(BINS):
        angle = ((n * (FIRST + k)) % SAMPLES) * (2.0 * math.pi / SAMPLES)
        table[k, 0] = np.cos(angle)
        table[k, 1] = -np.sin(angle)
    return table.reshape(BINGROUPS * ROWS, SAMPLES).astype(ml_dtypes.bfloat16)


def _inverse_const():
    tau = np.arange(LAGS) - LAGS // 2
    table = np.zeros((BINGROUPS * QN, 2, LAGS), np.float32)
    for k in range(BINS):
        angle = (((FIRST + k) * tau) % SAMPLES) * (2.0 * math.pi / SAMPLES)
        table[k, 0] = np.cos(angle)
        table[k, 1] = -np.sin(angle)
    table = table.reshape(BINGROUPS, GROUPS, 4, 2, LAGS)
    out = np.zeros((BINGROUPS, 4, PART, GROUPS, 4, 2, 16), np.float32)
    for b4 in range(4):
        for i4 in range(4):
            rows = np.moveaxis(table, -1, 1)
            out[:, b4, i4 * LAGS : (i4 + 1) * LAGS, :, :, :, b4 * 4 + i4] = rows
    return out.reshape(BINGROUPS, 4 * PART, GROUPS * 128).astype(ml_dtypes.bfloat16)


def _select_const():
    out = np.zeros((PART, 512), np.float32)
    for i4 in range(4):
        for lag in range(LAGS):
            out[i4 * LAGS + lag, i4 * 128 + lag] = 1.0
    return out.astype(ml_dtypes.bfloat16)


def _main_kernel(widths_hbm, wave_hbm, fwd_hbm, inv_all, select_hbm, out, *scratch):
    widths, wave, fwd, sb, rb, g, wt, kt, ct = scratch[:9]
    parts, theirs, mine, pair_out, pair_in, outer, final, select = scratch[9:17]
    (in_sem, a_send, a_recv, o_send, o_recv, g_send, g_recv, r_send, r_recv) = scratch[17:]
    f32, bf16 = jnp.float32, jnp.bfloat16

    band = lax.axis_index("band")
    tile = lax.axis_index("tile")
    core = lax.rem(band, 2)
    zh = band // 2
    z = lax.rem(tile, 2)
    side = band // 4
    group = lax.rem(band, BINGROUPS)
    home = z == side
    y = lax.rem(tile // 2, 8)
    first = (7 - y) // 7
    last = (y + 1) // 8

    def at_band(b):
        return {"band": b, "tile": tile}

    def at_tile(t):
        return {"band": band, "tile": lax.rem(t + TILE, TILE)}

    barrier = pltpu.get_barrier_semaphore()
    peers = [at_band(lax.rem(band + o, BAND)) for o in range(1, BAND)]
    other_z = tile + 1 - 2 * z
    above, below = tile + 2 - 16 * last, tile - 2 + 16 * first
    peers += [at_tile(t) for t in (tile + 16, tile - 16, tile + 32)]
    peers += [at_tile(t) for t in (tile + 2, tile - 2, above, below)]
    for peer in peers:
        pl.semaphore_signal(barrier, inc=1, device_id=peer, device_id_type=MESH)

    @pl.when(jnp.logical_not(home))
    def _():
        for b in range(BAND):
            peer = {"band": b, "tile": other_z}
            pl.semaphore_signal(barrier, inc=1, device_id=peer, device_id_type=MESH)

    wave_copy = pltpu.make_async_copy(wave_hbm, wave, in_sem.at[0])
    fwd_copy = pltpu.make_async_copy(fwd_hbm, fwd, in_sem.at[1])
    widths_copy = pltpu.make_async_copy(widths_hbm, widths, in_sem.at[2])
    kt_copy = pltpu.make_async_copy(inv_all.at[group], kt, in_sem.at[3])
    select_copy = pltpu.make_async_copy(select_hbm, select, in_sem.at[4])
    for copy in (wave_copy, fwd_copy, widths_copy, kt_copy, select_copy):
        copy.start()
    wave_copy.wait()
    fwd_copy.wait()
    widths_copy.wait()

    nt = (((1,), (1,)), ((), ()))
    samples = jnp.concatenate([wave[:, s, :] for s in range(SEGL)], axis=0)
    spectra = lax.dot_general(fwd[...], samples, nt, preferred_element_type=f32).astype(bf16)
    values = spectra.astype(f32)
    squares = values * values
    sq_hi = squares.astype(bf16)
    sq_lo = (squares - sq_hi.astype(f32)).astype(bf16)
    offsets = []
    total = widths[0] * 0
    for b in range(BAND):
        offsets.append(total)
        total = total + widths[b]

    def member(rows, bins):
        low = jnp.zeros(rows.shape, jnp.int32)
        size = jnp.zeros(rows.shape, jnp.int32)
        for b in range(BAND):
            low = jnp.where(rows == b, offsets[b], low)
            size = jnp.where(rows == b, widths[b], size)
        return jnp.where((bins >= low) & (bins < low + size), 1.0, 0.0).astype(f32)

    shape = (BAND, BINGROUPS * ROWS)
    is_in = member(
        lax.broadcasted_iota(jnp.int32, shape, 0), lax.broadcasted_iota(jnp.int32, shape, 1) // 2
    ).astype(bf16)
    part = jnp.dot(is_in, sq_hi, preferred_element_type=f32)
    part = part + jnp.dot(is_in, sq_lo, preferred_element_type=f32)
    part_hi = part.astype(bf16).astype(f32)
    energies = jnp.concatenate([part_hi, part - part_hi], axis=0).astype(bf16)
    for b in range(BINGROUPS):
        sb[b, :ROWS] = spectra[b * ROWS : (b + 1) * ROWS]
        sb[b, ROWS:] = energies
    rb[0, 0] = sb[group]

    pl.semaphore_wait(barrier, len(peers) + BINGROUPS)

    exchange = []
    for o in range(1, BAND):
        to = lax.rem(band + o, BAND)
        copy = pltpu.make_async_remote_copy(
            src_ref=sb.at[lax.rem(to, BINGROUPS)],
            dst_ref=rb.at[0, o],
            send_sem=a_send.at[o],
            recv_sem=a_recv.at[o],
            device_id=at_band(to),
            device_id_type=MESH,
        )
        copy.start()
        exchange.append(copy)
    across = []
    for j in range(BINGROUPS):
        to = 4 * z + j
        o = lax.rem(to - band + BAND, BAND)
        copy = pltpu.make_async_remote_copy(
            src_ref=sb.at[j],
            dst_ref=rb.at[1, o],
            send_sem=o_send.at[j],
            recv_sem=o_recv.at[o],
            device_id={"band": to, "tile": other_z},
            device_id_type=MESH,
        )
        copy.start()
        across.append(copy)

    lane = lax.broadcasted_iota(jnp.int32, (CH, 128), 1)

    def whiten(which):
        energy = jnp.zeros((BAND, 128), f32)
        for o in range(BAND):
            tail = rb[which, o, ROWS:].astype(f32)
            energy = energy + tail[:BAND] + tail[BAND:]
        energy = energy + pltpu.roll(energy, 64, 1)
        energy = energy + pltpu.roll(energy, 32, 1)
        row8 = lax.broadcasted_iota(jnp.int32, (BAND, 128), 0)
        width8 = jnp.ones((BAND, 128), f32)
        for b in range(BAND):
            width8 = jnp.where(row8 == b, widths[b].astype(f32), width8)
        gain = lax.rsqrt(energy / (SEG * width8) + EPS)
        bins = group * QN + lax.broadcasted_iota(jnp.int32, (ROWS, 128), 0) // 2
        gains = jnp.zeros((ROWS, 128), f32)
        for b in range(BAND):
            inside = (bins >= offsets[b]) & (bins < offsets[b] + widths[b])
            gains = jnp.where(inside, gain[b : b + 1, :], gains)
        white = [
            (rb[which, o, :ROWS].astype(f32) * gains).astype(bf16).astype(f32) for o in range(BAND)
        ]
        tiles = []
        for pair in range(GROUPS // 2):
            stack = jnp.concatenate(
                [
                    white[o][(2 * pair + h) * 8 : (2 * pair + h + 1) * 8]
                    for h in range(2)
                    for o in range(BAND)
                ],
                axis=0,
            )
            flipped = jnp.transpose(stack)
            rolled = pltpu.roll(flipped, 64, 1)
            seg = [flipped[s * CH : (s + 1) * CH] for s in range(SEGL)]
            seg_r = [rolled[s * CH : (s + 1) * CH] for s in range(SEGL)]
            for low, high in ((seg, seg_r), (seg_r, seg)):
                tiles.append([jnp.where(lane < 64, low[2 * v], high[2 * v + 1]) for v in range(2)])
        return tiles

    for copy in exchange:
        copy.wait_recv()

    @pl.when(jnp.logical_not(home))
    def _():
        for o in range(BAND):
            pltpu.make_async_remote_copy(
                src_ref=sb.at[0],
                dst_ref=rb.at[1, o],
                send_sem=o_send.at[0],
                recv_sem=o_recv.at[o],
                device_id={"band": band, "tile": other_z},
                device_id_type=MESH,
            ).wait_recv()

    for n, halves in enumerate(whiten(lax.rem(z + side, 2))):
        for v in range(2):
            first_lane = n % (GROUPS // 2) * 256 + v * 128
            g[n // (GROUPS // 2), :CH, first_lane : first_lane + 128] = halves[v].astype(bf16)

    def slot(r, h, instead=None, when=None):
        row = POS[r] * CH
        if instead is not None:
            row = pl.multiple_of(row + when * (POS[instead] - POS[r]) * CH, CH)
        return g.at[h, pl.ds(row, CH)]

    copies = {}

    def describe(name, src, dst, to):
        n = len(copies)
        copies[name] = pltpu.make_async_remote_copy(
            src_ref=src,
            dst_ref=dst,
            send_sem=g_send.at[n],
            recv_sem=g_recv.at[n],
            device_id=at_tile(to),
            device_id_type=MESH,
        )

    for h in range(2):
        describe((8, h), slot(0, h), slot(8, h), tile + 16)
        describe((16, h), slot(0, h), slot(16, h), tile + 32)
        for k in range(1, 5):
            describe((k, h), slot(k - 1, h, 7 + k, last), slot(k, h), above)
            if k < 4:
                describe((8 - k, h), slot(9 - k, h), slot(8 - k, h), tile - 2)
            if 1 < k < 4:
                describe((8 + k, h), slot(7 + k, h), slot(8 + k, h), tile + 2)
            if k > 1:
                describe((16 - k, h), slot(17 - k, h, 9 - k, first), slot(16 - k, h), below)
        describe((9, h), slot(1, h), slot(9, h), tile + 16)
        describe((15, h), slot(7, h), slot(15, h), tile + 16)

    def arrive(r, h):
        def start(other):
            copies[(other, h)].start()

        if r:
            copies[(r, h)].wait_recv()
        if r == 0:
            pl.when(last == 0)(lambda: start(1))
            start(8)
        elif r == 8:
            pl.when(last == 1)(lambda: start(1))
            start(7)
        elif r < 4:
            pl.when(last == 0)(lambda: start(r + 1))
            if r == 1:
                start(9)
        elif 4 < r < 8:
            if r > 5:
                start(r - 1)
            pl.when(first == 1)(lambda: start(r + 7))
            if r == 7:
                start(15)
        elif 8 < r < 12:
            pl.when(last == 1)(lambda: start(r - 7))
            if r < 11:
                start(r + 1)
        elif 12 < r < 16:
            pl.when(first == 0)(lambda: start(r - 1))

    arrive(0, 0)
    arrive(0, 1)
    for h in range(2):
        copies[(16, h)].start()

    even = lax.rem(lane, 2) == 0
    bin4 = lax.rem(lane // 2, 4)
    for n, halves in enumerate(whiten(0)):
        for v in range(2):
            own = halves[v]
            alt = jnp.where(even, pltpu.roll(own, 127, 1), -pltpu.roll(own, 1, 1))
            for q in range(4):
                for p in range(2):
                    kept = jnp.where(bin4 == q, own if p == 0 else alt, 0.0).astype(bf16)
                    for h in range(2):
                        row = h * 128 + q * 32 + p * 16
                        wt[n, row : row + 16, v * 128 : (v + 1) * 128] = kept[h * 16 : h * 16 + 16]

    wide = lax.broadcasted_iota(jnp.int32, (PART, 128), 1)

    def compute(k):
        start, blocks = CHUNKS[k]
        rows = PACKED[blocks]
        for n in range(GROUPS):
            low = n % (GROUPS // 2) * 256
            block = g[n // (GROUPS // 2), start * CH : (start + blocks) * CH, low : low + 256]
            block = jnp.concatenate([block] * (4 // blocks), axis=0)
            cross = lax.dot_general(wt[n], block, nt, preferred_element_type=f32).astype(bf16)
            for h in range(2):
                ct[n * 128 : (n + 1) * 128, h * 128 : (h + 1) * 128] = cross[h * 128 : (h + 1) * 128]
        lags = jnp.dot(kt[...], ct[...], preferred_element_type=f32) * SCALE
        for h in range(2):
            for b4 in range(4):
                share = lags[b4 * PART : (b4 + 1) * PART, h * 128 : (h + 1) * 128]
                if blocks < 4:
                    copies_of = 4 // blocks
                    step = (PART - rows) // (copies_of - 1)
                    packed = share[:rows]
                    for i in range(1, copies_of):
                        here = wide[:rows] // (32 * blocks) == i
                        packed = jnp.where(here, share[i * step : i * step + rows], packed)
                    share = packed
                parts[k, b4 % 2, 2 * h + b4 // 2, :rows] = share.astype(bf16)

    def place(k, region, share):
        start, blocks = CHUNKS[k]
        rows = PACKED[blocks]
        if blocks < 4:
            copies_of = 4 // blocks
            step = (PART - rows) // (copies_of - 1)
            pieces = [share]
            for i in range(1, copies_of):
                pieces.append(pltpu.roll(share, 128 - 32 * blocks * i, 1)[rows - step :])
            share = jnp.concatenate(pieces, axis=0)
        turned = lax.dot_general(
            share.astype(bf16), select[...], (((0,), (0,)), ((), ())), preferred_element_type=f32
        ).astype(bf16)
        for b in range(blocks):
            for i4 in range(4):
                lags = turned[b * CH : (b + 1) * CH, i4 * 128 : i4 * 128 + LAGS]
                out[region * 17 + start + b, i4] = lags

    adding = {}

    def send(name, n, k, src, dst, to):
        copy = pltpu.make_async_remote_copy(
            src_ref=src,
            dst_ref=dst,
            send_sem=r_send.at[k * 4 + n],
            recv_sem=r_recv.at[k * 4 + n],
            device_id=at_band(to),
            device_id_type=MESH,
        )
        copy.start()
        adding[(name, k)] = copy

    odd = lax.rem(zh, 2)
    mate, beyond, far = zh + 1 - 2 * odd, lax.rem(zh + 2 * odd + 3, 4), lax.rem(zh + 2, 4)
    to_sibling, to_mate, to_beyond = 2 * zh + 1 - core, 2 * mate + core, 2 * beyond + core
    to_far = 2 * far + core

    def r0(k):
        compute(k)
        rows = pl.ds(0, PACKED[CHUNKS[k][1]])
        send("sib", 0, k, parts.at[k, 1 - core, :, rows], theirs.at[k, :, rows], to_sibling)

    def r1(k):
        rows = PACKED[CHUNKS[k][1]]
        adding[("sib", k)].wait_recv()

        def both(n):
            return parts[k, core, n, :rows].astype(f32) + theirs[k, n, :rows].astype(f32)

        cut = pl.ds(0, rows)
        if k in DIRECT:
            pair_out[k, 1, :rows] = both(far).astype(bf16)
            send("far", 3, k, pair_out.at[k, 1, cut], final.at[k, 1, cut], to_far)
            pair_out[k, 0, :rows] = both(mate).astype(bf16)
            send("pair", 1, k, pair_out.at[k, 0, cut], pair_in.at[k, 0, cut], to_mate)
            outer[k, :rows] = both(beyond).astype(bf16)
            send("out", 2, k, outer.at[k, cut], final.at[k, 0, cut], to_beyond)
        else:
            pair_out[k, 0, :rows] = both(mate).astype(bf16)
            pair_out[k, 1, :rows] = both(far).astype(bf16)
            send("pair", 1, k, pair_out.at[k, :, cut], pair_in.at[k, :, cut], to_mate)
            outer[k, :rows] = both(beyond).astype(bf16)
        mine[k, :rows] = both(zh).astype(bf16)

    def r2(k):
        rows = PACKED[CHUNKS[k][1]]
        adding[("pair", k)].wait_recv()
        if k not in DIRECT:
            passed = outer[k, :rows].astype(f32) + pair_in[k, 1, :rows].astype(f32)
            outer[k, :rows] = passed.astype(bf16)
            send("out", 2, k, outer.at[k, pl.ds(0, rows)], final.at[k, 0, pl.ds(0, rows)], to_beyond)
        place(k, 0, mine[k, :rows].astype(f32) + pair_in[k, 0, :rows].astype(f32))

    def r3(k):
        rows = PACKED[CHUNKS[k][1]]
        adding[("out", k)].wait_recv()
        whole = final[k, 0, :rows].astype(f32)
        if k in DIRECT:
            adding[("far", k)].wait_recv()
            whole = whole + final[k, 1, :rows].astype(f32)
        place(k, 1, whole)

    kt_copy.wait()
    select_copy.wait()
    stages = {"c": r0, "s": r1, "m": r2, "f": r3}
    arrive(8, 0)

    @pl.when(first == 1)
    def _():
        arrive(8, 1)
        arrive(1, 0)

    @pl.when(first == 0)
    def _():
        arrive(1, 0)
        arrive(8, 1)

    for step in STEPS:
        if step[0] in stages:
            stages[step[0]](int(step[1:]))
        else:
            arrive(int(step[:-1]), "ab".index(step[-1]))

    for copy in exchange + across:
        copy.wait_send()
    for copy in copies.values():
        copy.wait_send()
    for copy in adding.values():
        copy.wait_send()


def _place_kernel(table, place, turned, out, sems):
    tile = lax.axis_index("tile")
    side = lax.axis_index("band") // 4

    def copy(s):
        partner = table[0, s]
        behind = lax.rem(tile // 2 - partner // 2 + TILE // 2, TILE // 2)
        block = place[behind] + lax.rem(partner + side, 2) * 17
        return pltpu.make_async_copy(turned.at[block], out.at[s], sems.at[s])

    for s in range(out.shape[0]):
        copy(s).start()
    for s in range(out.shape[0]):
        copy(s).wait()


def body(waveforms, band_widths, pair_table):
    slots = pair_table.shape[1]
    bf16 = jnp.bfloat16
    scratch = [
        pltpu.SMEM((BAND,), jnp.int32),
        pltpu.VMEM(waveforms.shape, bf16),
        pltpu.VMEM((BINGROUPS * ROWS, SAMPLES), bf16),
        pltpu.VMEM((BINGROUPS, MSG, 128), bf16),
        pltpu.VMEM((2, BAND, MSG, 128), bf16),
        pltpu.VMEM((2, 17 * CH, WIDE // 2), bf16),
        pltpu.VMEM((GROUPS, 256, 256), bf16),
        pltpu.VMEM((4 * PART, GROUPS * 128), bf16),
        pltpu.VMEM((GROUPS * 128, 256), bf16),
        pltpu.VMEM((len(CHUNKS), 2, 4, PART, 128), bf16),
        pltpu.VMEM((len(CHUNKS), 4, PART, 128), bf16),
        pltpu.VMEM((len(CHUNKS), PART, 128), bf16),
        pltpu.VMEM((len(CHUNKS), 2, PART, 128), bf16),
        pltpu.VMEM((len(CHUNKS), 2, PART, 128), bf16),
        pltpu.VMEM((len(CHUNKS), PART, 128), bf16),
        pltpu.VMEM((len(CHUNKS), 2, PART, 128), bf16),
        pltpu.VMEM((PART, 512), bf16),
    ]
    dma = pltpu.SemaphoreType.DMA
    scratch += [
        dma((5,)),
        dma((BAND,)),
        dma((BAND,)),
        dma((BINGROUPS,)),
        dma((BAND,)),
        dma((32,)),
        dma((32,)),
        dma((4 * len(CHUNKS),)),
        dma((4 * len(CHUNKS),)),
    ]
    vmem = pl.BlockSpec(memory_space=pltpu.VMEM)
    smem = pl.BlockSpec(memory_space=pltpu.SMEM)
    summed = pl.pallas_call(
        _main_kernel,
        out_shape=jax.ShapeDtypeStruct((34, 4, CH, LAGS), bf16),
        in_specs=[pl.BlockSpec(memory_space=pl.ANY)] * 5,
        out_specs=vmem,
        scratch_shapes=scratch,
        compiler_params=pltpu.CompilerParams(
            collective_id=0, has_side_effects=True, vmem_limit_bytes=60 * 1024 * 1024
        ),
        name="correlate",
    )(
        band_widths,
        waveforms,
        jnp.asarray(_forward_const()),
        jnp.asarray(_inverse_const()),
        jnp.asarray(_select_const()),
    )
    place = np.zeros((TILE // 2,), np.int32)
    for r, i in POS.items():
        place[r] = i
    placed = pl.pallas_call(
        _place_kernel,
        out_shape=jax.ShapeDtypeStruct((slots, 4, CH, LAGS), bf16),
        in_specs=[smem, smem, pl.BlockSpec(memory_space=pl.ANY)],
        out_specs=pl.BlockSpec(memory_space=pl.ANY),
        scratch_shapes=[pltpu.SemaphoreType.DMA((slots,))],
        compiler_params=pltpu.CompilerParams(vmem_limit_bytes=60 * 1024 * 1024),
        name="place",
    )(pair_table, jnp.asarray(place), summed)
    return placed[None]


def solution(mesh):
    placed = (P("tile", "band", None), P(), P("tile", None))
    return jax.shard_map(
        body,
        mesh=mesh,
        in_specs=placed,
        out_specs=P("tile", None, "band", None, None),
        check_vma=False,
    )
```

```python
import functools
import math

import jax
import jax.numpy as jnp
import ml_dtypes
import numpy as np
from jax import lax
from jax.experimental import pallas as pl
from jax.experimental.pallas import tpu as pltpu
from jax.sharding import PartitionSpec as P

BINS = 180
FIRST = 20
LAGS = 51
SAMPLES = 500
EPS = 1e-05

BAND = 8
TILE = 64
CH = 32
SEG = 32
SEGL = 4
QN = 48
BINGROUPS = 4
GROUPS = QN // 4
ROWS = 2 * QN
MSG = ROWS + 16
WIDE = QN * 64
PART = 208
SCALE = 1.0 / math.sqrt(SEG * BINS)
MESH = pl.DeviceIdType.MESH

ORDER = [0, 8, 16, 1, 7, 9, 15, 2, 6, 10, 14, 3, 5, 11, 13, 4, 12]
POS = {r: i for i, r in enumerate(ORDER)}
CHUNKS = [(0, 4), (4, 4), (8, 4), (12, 2), (14, 2), (16, 1)]
PACKED = {4: PART, 2: 112, 1: 64}
DIRECT = (4, 5)
STEPS = [
    "1b", "7a", "9a", "16a", "16b", "7b", "9b", "c0",
    "2a", "15a", "s0", "2b", "15b", "10a", "10b", "6a", "c1",
    "3a", "s1", "6b", "14a", "3b", "14b", "c2",
    "5a", "m0", "11b", "11a", "5b", "s2", "c3",
    "13a", "4a", "m1", "s3", "4b", "13b", "c4",
    "s4", "12a", "m2", "12b", "c5",
    "m3", "s5", "f0", "f1", "f2", "f3", "m4", "f4", "m5", "f5",
]


def _forward_const():
    n = np.arange(SAMPLES)
    table = np.zeros((BINGROUPS * QN, 2, SAMPLES), np.float32)
    for k in range(BINS):
        angle = ((n * (FIRST + k)) % SAMPLES) * (2.0 * math.pi / SAMPLES)
        table[k, 0] = np.cos(angle)
        table[k, 1] = -np.sin(angle)
    return table.reshape(BINGROUPS * ROWS, SAMPLES).astype(ml_dtypes.bfloat16)


def _inverse_const():
    tau = np.arange(LAGS) - LAGS // 2
    table = np.zeros((BINGROUPS * QN, 2, LAGS), np.float32)
    for k in range(BINS):
        angle = (((FIRST + k) * tau) % SAMPLES) * (2.0 * math.pi / SAMPLES)
        table[k, 0] = np.cos(angle)
        table[k, 1] = -np.sin(angle)
    table = table.reshape(BINGROUPS, GROUPS, 4, 2, LAGS)
    out = np.zeros((BINGROUPS, 4, PART, GROUPS, 4, 2, 16), np.float32)
    for b4 in range(4):
        for i4 in range(4):
            rows = np.moveaxis(table, -1, 1)
            out[:, b4, i4 * LAGS : (i4 + 1) * LAGS, :, :, :, b4 * 4 + i4] = rows
    return out.reshape(BINGROUPS, 4 * PART, GROUPS * 128).astype(ml_dtypes.bfloat16)


def _select_const():
    out = np.zeros((PART, 512), np.float32)
    for i4 in range(4):
        for lag in range(LAGS):
            out[i4 * LAGS + lag, i4 * 128 + lag] = 1.0
    return out.astype(ml_dtypes.bfloat16)


def _main_kernel(widths_hbm, wave_hbm, fwd_hbm, inv_all, select_hbm, out, *scratch):
    widths, wave, fwd, sb, rb, g, wt, kt, ct = scratch[:9]
    parts, theirs, mine, pair_out, pair_in, outer, final, select = scratch[9:17]
    (in_sem, a_send, a_recv, o_recv, g_send, g_recv, r_send, r_recv) = scratch[17:]
    f32, bf16 = jnp.float32, jnp.bfloat16

    band = lax.axis_index("band")
    tile = lax.axis_index("tile")
    core = lax.rem(band, 2)
    zh = band // 2
    z = lax.rem(tile, 2)
    side = band // 4
    group = lax.rem(band, BINGROUPS)
    home = z == side
    y = lax.rem(tile // 2, 8)
    first = (7 - y) // 7
    last = (y + 1) // 8

    def at_band(b):
        return {"band": b, "tile": tile}

    def at_tile(t):
        return {"band": band, "tile": lax.rem(t + TILE, TILE)}

    barrier = pltpu.get_barrier_semaphore()
    peers = [at_band(lax.rem(band + o, BAND)) for o in range(1, BAND)]
    other_z = tile + 1 - 2 * z
    above, below = tile + 2 - 16 * last, tile - 2 + 16 * first
    peers += [at_tile(t) for t in (tile + 16, tile - 16, tile + 32)]
    peers += [at_tile(t) for t in (tile + 2, tile - 2, above, below)]
    for peer in peers:
        pl.semaphore_signal(barrier, inc=1, device_id=peer, device_id_type=MESH)

    @pl.when(jnp.logical_not(home))
    def _():
        for b in range(BAND):
            peer = {"band": b, "tile": other_z}
            pl.semaphore_signal(barrier, inc=1, device_id=peer, device_id_type=MESH)

    wave_copy = pltpu.make_async_copy(wave_hbm, wave, in_sem.at[0])
    fwd_copy = pltpu.make_async_copy(fwd_hbm, fwd, in_sem.at[1])
    widths_copy = pltpu.make_async_copy(widths_hbm, widths, in_sem.at[2])
    kt_copy = pltpu.make_async_copy(inv_all.at[group], kt, in_sem.at[3])
    select_copy = pltpu.make_async_copy(select_hbm, select, in_sem.at[4])
    for copy in (wave_copy, fwd_copy, widths_copy, kt_copy, select_copy):
        copy.start()
    wave_copy.wait()
    fwd_copy.wait()
    widths_copy.wait()

    nt = (((1,), (1,)), ((), ()))
    samples = jnp.concatenate([wave[:, s, :] for s in range(SEGL)], axis=0)
    spectra = lax.dot_general(fwd[...], samples, nt, preferred_element_type=f32).astype(bf16)
    values = spectra.astype(f32)
    squares = values * values
    sq_hi = squares.astype(bf16)
    sq_lo = (squares - sq_hi.astype(f32)).astype(bf16)
    offsets = []
    total = widths[0] * 0
    for b in range(BAND):
        offsets.append(total)
        total = total + widths[b]

    def member(rows, bins):
        low = jnp.zeros(rows.shape, jnp.int32)
        size = jnp.zeros(rows.shape, jnp.int32)
        for b in range(BAND):
            low = jnp.where(rows == b, offsets[b], low)
            size = jnp.where(rows == b, widths[b], size)
        return jnp.where((bins >= low) & (bins < low + size), 1.0, 0.0).astype(f32)

    shape = (BAND, BINGROUPS * ROWS)
    is_in = member(
        lax.broadcasted_iota(jnp.int32, shape, 0), lax.broadcasted_iota(jnp.int32, shape, 1) // 2
    ).astype(bf16)
    part = jnp.dot(is_in, sq_hi, preferred_element_type=f32)
    part = part + jnp.dot(is_in, sq_lo, preferred_element_type=f32)
    part_hi = part.astype(bf16).astype(f32)
    energies = jnp.concatenate([part_hi, part - part_hi], axis=0).astype(bf16)
    for b in range(BINGROUPS):
        sb[b, :ROWS] = spectra[b * ROWS : (b + 1) * ROWS]
        sb[b, ROWS:] = energies
    rb[0, 0] = sb[group]

    pl.semaphore_wait(barrier, len(peers) + BINGROUPS)

    exchange = []

    def share(n, to, tile_to, which, sems):
        o = lax.rem(to - band + BAND, BAND)
        copy = pltpu.make_async_remote_copy(
            src_ref=sb.at[lax.rem(to, BINGROUPS)],
            dst_ref=rb.at[which, o],
            send_sem=a_send.at[n],
            recv_sem=sems.at[o],
            device_id={"band": to, "tile": tile_to},
            device_id_type=MESH,
        )
        if which:
            copy.start()
        else:
            pl.when(to != band)(copy.start)
        exchange.append((to, which, copy))

    for j in range(BINGROUPS):
        share(j, 4 * z + j, tile, 0, a_recv)
        share(4 + j, 4 * z + j, other_z, 1, o_recv)
    for j in range(BINGROUPS):
        share(8 + j, 4 - 4 * z + j, tile, 0, a_recv)

    def collect(which):
        for o in range(1 - which, BAND):
            pltpu.make_async_remote_copy(
                src_ref=sb.at[0],
                dst_ref=rb.at[which, o],
                send_sem=a_send.at[0],
                recv_sem=(o_recv if which else a_recv).at[o],
                device_id={"band": band, "tile": other_z},
                device_id_type=MESH,
            ).wait_recv()

    lane = lax.broadcasted_iota(jnp.int32, (CH, 128), 1)

    def whiten(which):
        energy = jnp.zeros((BAND, 128), f32)
        for o in range(BAND):
            tail = rb[which, o, ROWS:].astype(f32)
            energy = energy + tail[:BAND] + tail[BAND:]
        energy = energy + pltpu.roll(energy, 64, 1)
        energy = energy + pltpu.roll(energy, 32, 1)
        row8 = lax.broadcasted_iota(jnp.int32, (BAND, 128), 0)
        width8 = jnp.ones((BAND, 128), f32)
        for b in range(BAND):
            width8 = jnp.where(row8 == b, widths[b].astype(f32), width8)
        gain = lax.rsqrt(energy / (SEG * width8) + EPS)
        bins = group * QN + lax.broadcasted_iota(jnp.int32, (ROWS, 128), 0) // 2
        gains = jnp.zeros((ROWS, 128), f32)
        for b in range(BAND):
            inside = (bins >= offsets[b]) & (bins < offsets[b] + widths[b])
            gains = jnp.where(inside, gain[b : b + 1, :], gains)
        white = [
            (rb[which, o, :ROWS].astype(f32) * gains).astype(bf16).astype(f32) for o in range(BAND)
        ]
        tiles = []
        for pair in range(GROUPS // 2):
            stack = jnp.concatenate(
                [
                    white[o][(2 * pair + h) * 8 : (2 * pair + h + 1) * 8]
                    for h in range(2)
                    for o in range(BAND)
                ],
                axis=0,
            )
            flipped = jnp.transpose(stack)
            rolled = pltpu.roll(flipped, 64, 1)
            seg = [flipped[s * CH : (s + 1) * CH] for s in range(SEGL)]
            seg_r = [rolled[s * CH : (s + 1) * CH] for s in range(SEGL)]
            for low, high in ((seg, seg_r), (seg_r, seg)):
                tiles.append([jnp.where(lane < 64, low[2 * v], high[2 * v + 1]) for v in range(2)])
        return tiles

    pl.when(home)(lambda: collect(0))
    pl.when(jnp.logical_not(home))(lambda: collect(1))
    for n, halves in enumerate(whiten(lax.rem(z + side, 2))):
        for v in range(2):
            first_lane = n % (GROUPS // 2) * 256 + v * 128
            g[n // (GROUPS // 2), :CH, first_lane : first_lane + 128] = halves[v].astype(bf16)

    def slot(r, h, instead=None, when=None):
        row = POS[r] * CH
        if instead is not None:
            row = pl.multiple_of(row + when * (POS[instead] - POS[r]) * CH, CH)
        return g.at[h, pl.ds(row, CH)]

    copies = {}

    def describe(name, src, dst, to):
        n = len(copies)
        copies[name] = pltpu.make_async_remote_copy(
            src_ref=src,
            dst_ref=dst,
            send_sem=g_send.at[n],
            recv_sem=g_recv.at[n],
            device_id=at_tile(to),
            device_id_type=MESH,
        )

    for h in range(2):
        describe((8, h), slot(0, h), slot(8, h), tile + 16)
        describe((16, h), slot(0, h), slot(16, h), tile + 32)
        for k in range(1, 5):
            describe((k, h), slot(k - 1, h, 7 + k, last), slot(k, h), above)
            if k < 4:
                describe((8 - k, h), slot(9 - k, h), slot(8 - k, h), tile - 2)
            if 1 < k < 4:
                describe((8 + k, h), slot(7 + k, h), slot(8 + k, h), tile + 2)
            if k > 1:
                describe((16 - k, h), slot(17 - k, h, 9 - k, first), slot(16 - k, h), below)
        describe((9, h), slot(1, h), slot(9, h), tile + 16)
        describe((15, h), slot(7, h), slot(15, h), tile + 16)

    def arrive(r, h):
        def start(other):
            copies[(other, h)].start()

        if r:
            copies[(r, h)].wait_recv()
        if r == 0:
            pl.when(last == 0)(lambda: start(1))
            start(8)
        elif r == 8:
            pl.when(last == 1)(lambda: start(1))
            start(7)
        elif r < 4:
            pl.when(last == 0)(lambda: start(r + 1))
            if r == 1:
                start(9)
        elif 4 < r < 8:
            if r > 5:
                start(r - 1)
            pl.when(first == 1)(lambda: start(r + 7))
            if r == 7:
                start(15)
        elif 8 < r < 12:
            pl.when(last == 1)(lambda: start(r - 7))
            if r < 11:
                start(r + 1)
        elif 12 < r < 16:
            pl.when(first == 0)(lambda: start(r - 1))

    arrive(0, 0)
    arrive(0, 1)
    for h in range(2):
        copies[(16, h)].start()

    even = lax.rem(lane, 2) == 0
    bin4 = lax.rem(lane // 2, 4)
    pl.when(jnp.logical_not(home))(lambda: collect(0))
    for n, halves in enumerate(whiten(0)):
        for v in range(2):
            own = halves[v]
            alt = jnp.where(even, pltpu.roll(own, 127, 1), -pltpu.roll(own, 1, 1))
            for q in range(4):
                for p in range(2):
                    kept = jnp.where(bin4 == q, own if p == 0 else alt, 0.0).astype(bf16)
                    for h in range(2):
                        row = h * 128 + q * 32 + p * 16
                        wt[n, row : row + 16, v * 128 : (v + 1) * 128] = kept[h * 16 : h * 16 + 16]

    wide = lax.broadcasted_iota(jnp.int32, (PART, 128), 1)

    def compute(k):
        start, blocks = CHUNKS[k]
        rows = PACKED[blocks]
        for n in range(GROUPS):
            low = n % (GROUPS // 2) * 256
            block = g[n // (GROUPS // 2), start * CH : (start + blocks) * CH, low : low + 256]
            block = jnp.concatenate([block] * (4 // blocks), axis=0)
            cross = lax.dot_general(wt[n], block, nt, preferred_element_type=f32).astype(bf16)
            for h in range(2):
                ct[n * 128 : (n + 1) * 128, h * 128 : (h + 1) * 128] = cross[h * 128 : (h + 1) * 128]
        lags = jnp.dot(kt[...], ct[...], preferred_element_type=f32) * SCALE
        for h in range(2):
            for b4 in range(4):
                share = lags[b4 * PART : (b4 + 1) * PART, h * 128 : (h + 1) * 128]
                if blocks < 4:
                    copies_of = 4 // blocks
                    step = (PART - rows) // (copies_of - 1)
                    packed = share[:rows]
                    for i in range(1, copies_of):
                        here = wide[:rows] // (32 * blocks) == i
                        packed = jnp.where(here, share[i * step : i * step + rows], packed)
                    share = packed
                parts[k, b4 % 2, 2 * h + b4 // 2, :rows] = share.astype(bf16)

    def place(k, region, share):
        start, blocks = CHUNKS[k]
        rows = PACKED[blocks]
        if blocks < 4:
            copies_of = 4 // blocks
            step = (PART - rows) // (copies_of - 1)
            pieces = [share]
            for i in range(1, copies_of):
                pieces.append(pltpu.roll(share, 128 - 32 * blocks * i, 1)[rows - step :])
            share = jnp.concatenate(pieces, axis=0)
        turned = lax.dot_general(
            share.astype(bf16), select[...], (((0,), (0,)), ((), ())), preferred_element_type=f32
        ).astype(bf16)
        for b in range(blocks):
            for i4 in range(4):
                lags = turned[b * CH : (b + 1) * CH, i4 * 128 : i4 * 128 + LAGS]
                out[region * 17 + start + b, i4] = lags

    adding = {}

    def send(name, n, k, src, dst, to):
        copy = pltpu.make_async_remote_copy(
            src_ref=src,
            dst_ref=dst,
            send_sem=r_send.at[k * 4 + n],
            recv_sem=r_recv.at[k * 4 + n],
            device_id=at_band(to),
            device_id_type=MESH,
        )
        copy.start()
        adding[(name, k)] = copy

    odd = lax.rem(zh, 2)
    mate, beyond, far = zh + 1 - 2 * odd, lax.rem(zh + 2 * odd + 3, 4), lax.rem(zh + 2, 4)
    to_sibling, to_mate, to_beyond = 2 * zh + 1 - core, 2 * mate + core, 2 * beyond + core
    to_far = 2 * far + core

    def r0(k):
        compute(k)
        rows = pl.ds(0, PACKED[CHUNKS[k][1]])
        send("sib", 0, k, parts.at[k, 1 - core, :, rows], theirs.at[k, :, rows], to_sibling)

    def r1(k):
        rows = PACKED[CHUNKS[k][1]]
        adding[("sib", k)].wait_recv()

        def both(n):
            return parts[k, core, n, :rows].astype(f32) + theirs[k, n, :rows].astype(f32)

        cut = pl.ds(0, rows)
        if k in DIRECT:
            pair_out[k, 1, :rows] = both(far).astype(bf16)
            send("far", 3, k, pair_out.at[k, 1, cut], final.at[k, 1, cut], to_far)
            pair_out[k, 0, :rows] = both(mate).astype(bf16)
            send("pair", 1, k, pair_out.at[k, 0, cut], pair_in.at[k, 0, cut], to_mate)
            outer[k, :rows] = both(beyond).astype(bf16)
            send("out", 2, k, outer.at[k, cut], final.at[k, 0, cut], to_beyond)
        else:
            pair_out[k, 0, :rows] = both(mate).astype(bf16)
            pair_out[k, 1, :rows] = both(far).astype(bf16)
            send("pair", 1, k, pair_out.at[k, :, cut], pair_in.at[k, :, cut], to_mate)
            outer[k, :rows] = both(beyond).astype(bf16)
        mine[k, :rows] = both(zh).astype(bf16)

    def r2(k):
        rows = PACKED[CHUNKS[k][1]]
        adding[("pair", k)].wait_recv()
        if k not in DIRECT:
            passed = outer[k, :rows].astype(f32) + pair_in[k, 1, :rows].astype(f32)
            outer[k, :rows] = passed.astype(bf16)
            send("out", 2, k, outer.at[k, pl.ds(0, rows)], final.at[k, 0, pl.ds(0, rows)], to_beyond)
        place(k, 0, mine[k, :rows].astype(f32) + pair_in[k, 0, :rows].astype(f32))

    def r3(k):
        rows = PACKED[CHUNKS[k][1]]
        adding[("out", k)].wait_recv()
        whole = final[k, 0, :rows].astype(f32)
        if k in DIRECT:
            adding[("far", k)].wait_recv()
            whole = whole + final[k, 1, :rows].astype(f32)
        place(k, 1, whole)

    kt_copy.wait()
    select_copy.wait()
    stages = {"c": r0, "s": r1, "m": r2, "f": r3}
    arrive(8, 0)

    @pl.when(first == 1)
    def _():
        arrive(8, 1)
        arrive(1, 0)

    @pl.when(first == 0)
    def _():
        arrive(1, 0)
        arrive(8, 1)

    for step in STEPS:
        if step[0] in stages:
            stages[step[0]](int(step[1:]))
        else:
            arrive(int(step[:-1]), "ab".index(step[-1]))

    for to, which, copy in exchange:
        if which:
            copy.wait_send()
        else:
            pl.when(to != band)(copy.wait_send)
    for copy in copies.values():
        copy.wait_send()
    for copy in adding.values():
        copy.wait_send()


def _place_kernel(table, place, turned, out):
    tile = lax.axis_index("tile")
    side = lax.axis_index("band") // 4

    def step(s, carry):
        partner = table[0, s]
        behind = lax.rem(tile // 2 - partner // 2 + TILE // 2, TILE // 2)
        out[s] = turned[place[behind] + lax.rem(partner + side, 2) * 17]
        return carry

    lax.fori_loop(0, out.shape[0], step, 0)


def body(waveforms, band_widths, pair_table):
    slots = pair_table.shape[1]
    bf16 = jnp.bfloat16
    scratch = [
        pltpu.SMEM((BAND,), jnp.int32),
        pltpu.VMEM(waveforms.shape, bf16),
        pltpu.VMEM((BINGROUPS * ROWS, SAMPLES), bf16),
        pltpu.VMEM((BINGROUPS, MSG, 128), bf16),
        pltpu.VMEM((2, BAND, MSG, 128), bf16),
        pltpu.VMEM((2, 17 * CH, WIDE // 2), bf16),
        pltpu.VMEM((GROUPS, 256, 256), bf16),
        pltpu.VMEM((4 * PART, GROUPS * 128), bf16),
        pltpu.VMEM((GROUPS * 128, 256), bf16),
        pltpu.VMEM((len(CHUNKS), 2, 4, PART, 128), bf16),
        pltpu.VMEM((len(CHUNKS), 4, PART, 128), bf16),
        pltpu.VMEM((len(CHUNKS), PART, 128), bf16),
        pltpu.VMEM((len(CHUNKS), 2, PART, 128), bf16),
        pltpu.VMEM((len(CHUNKS), 2, PART, 128), bf16),
        pltpu.VMEM((len(CHUNKS), PART, 128), bf16),
        pltpu.VMEM((len(CHUNKS), 2, PART, 128), bf16),
        pltpu.VMEM((PART, 512), bf16),
    ]
    dma = pltpu.SemaphoreType.DMA
    scratch += [
        dma((5,)),
        dma((12,)),
        dma((BAND,)),
        dma((BAND,)),
        dma((32,)),
        dma((32,)),
        dma((4 * len(CHUNKS),)),
        dma((4 * len(CHUNKS),)),
    ]
    vmem = pl.BlockSpec(memory_space=pltpu.VMEM)
    smem = pl.BlockSpec(memory_space=pltpu.SMEM)
    summed = pl.pallas_call(
        _main_kernel,
        out_shape=jax.ShapeDtypeStruct((34, 4, CH, LAGS), bf16),
        in_specs=[pl.BlockSpec(memory_space=pl.ANY)] * 5,
        out_specs=vmem,
        scratch_shapes=scratch,
        compiler_params=pltpu.CompilerParams(
            collective_id=0, has_side_effects=True, vmem_limit_bytes=60 * 1024 * 1024
        ),
        name="correlate",
    )(
        band_widths,
        waveforms,
        jnp.asarray(_forward_const()),
        jnp.asarray(_inverse_const()),
        jnp.asarray(_select_const()),
    )
    place = np.zeros((TILE // 2,), np.int32)
    for r, i in POS.items():
        place[r] = i
    placed = pl.pallas_call(
        _place_kernel,
        out_shape=jax.ShapeDtypeStruct((slots, 4, CH, LAGS), bf16),
        in_specs=[smem, smem, vmem],
        out_specs=vmem,
        name="place",
    )(pair_table, jnp.asarray(place), summed)
    return placed[None]


def solution(mesh):
    placed = (P("tile", "band", None), P(), P("tile", None))
    return jax.shard_map(
        body,
        mesh=mesh,
        in_specs=placed,
        out_specs=P("tile", None, "band", None, None),
        check_vma=False,
    )
```

```python
import functools
import math

import jax
import jax.numpy as jnp
import ml_dtypes
import numpy as np
from jax import lax
from jax.experimental import pallas as pl
from jax.experimental.pallas import tpu as pltpu
from jax.sharding import PartitionSpec as P

BINS = 180
FIRST = 20
LAGS = 51
SAMPLES = 500
EPS = 1e-05

BAND = 8
TILE = 64
CH = 32
SEG = 32
SEGL = 4
QN = 48
BINGROUPS = 4
GROUPS = QN // 4
ROWS = 2 * QN
MSG = ROWS + 16
WIDE = QN * 64
PART = 208
SCALE = 1.0 / math.sqrt(SEG * BINS)
MESH = pl.DeviceIdType.MESH

ORDER = [0, 8, 16, 1, 7, 9, 15, 2, 6, 10, 14, 3, 5, 11, 13, 4, 12]
POS = {r: i for i, r in enumerate(ORDER)}
CHUNKS = [(0, 4), (4, 4), (8, 4), (12, 2), (14, 2), (16, 1)]
PACKED = {4: PART, 2: 112, 1: 64}
DIRECT = (4, 5)
STEPS = [
    "1b", "7a", "9a", "16a", "16b", "7b", "9b", "c0",
    "2a", "15a", "s0", "2b", "15b", "10a", "10b", "6a", "c1",
    "3a", "s1", "6b", "14a", "3b", "14b", "c2",
    "5a", "m0", "11b", "11a", "5b", "s2", "c3",
    "13a", "4a", "m1", "s3", "4b", "13b", "c4",
    "s4", "12a", "m2", "12b", "c5",
    "m3", "s5", "f0", "f1", "f2", "f3", "m4", "f4", "m5", "f5",
]


def _forward_const():
    n = np.arange(SAMPLES)
    table = np.zeros((BINGROUPS * QN, 2, SAMPLES), np.float32)
    for k in range(BINS):
        angle = ((n * (FIRST + k)) % SAMPLES) * (2.0 * math.pi / SAMPLES)
        table[k, 0] = np.cos(angle)
        table[k, 1] = -np.sin(angle)
    return table.reshape(BINGROUPS * ROWS, SAMPLES).astype(ml_dtypes.bfloat16)


def _inverse_const():
    tau = np.arange(LAGS) - LAGS // 2
    table = np.zeros((BINGROUPS * QN, 2, LAGS), np.float32)
    for k in range(BINS):
        angle = (((FIRST + k) * tau) % SAMPLES) * (2.0 * math.pi / SAMPLES)
        table[k, 0] = np.cos(angle)
        table[k, 1] = -np.sin(angle)
    table = table.reshape(BINGROUPS, GROUPS, 4, 2, LAGS)
    out = np.zeros((BINGROUPS, 2, PART, GROUPS, 4, 2, 8), np.float32)
    for b2 in range(2):
        for i4 in range(4):
            rows = np.moveaxis(table, -1, 1)
            out[:, b2, i4 * LAGS : (i4 + 1) * LAGS, :, :, :, b2 * 4 + i4] = rows
    return out.reshape(BINGROUPS, 2 * PART, GROUPS * 64).astype(ml_dtypes.bfloat16)


def _select_const():
    out = np.zeros((PART, 512), np.float32)
    for i4 in range(4):
        for lag in range(LAGS):
            out[i4 * LAGS + lag, i4 * 128 + lag] = 1.0
    return out.astype(ml_dtypes.bfloat16)


def _main_kernel(widths_hbm, wave_hbm, fwd_hbm, inv_all, select_hbm, out, *scratch):
    widths, wave, fwd, sb, rb, g, wt, kt, ct = scratch[:9]
    parts, theirs, mine, pair_out, pair_in, outer, final, select = scratch[9:17]
    (in_sem, a_send, a_recv, o_recv, g_send, g_recv, r_send, r_recv) = scratch[17:]
    f32, bf16 = jnp.float32, jnp.bfloat16

    band = lax.axis_index("band")
    tile = lax.axis_index("tile")
    core = lax.rem(band, 2)
    zh = band // 2
    z = lax.rem(tile, 2)
    side = band // 4
    group = lax.rem(band, BINGROUPS)
    home = z == side
    y = lax.rem(tile // 2, 8)
    first = (7 - y) // 7
    last = (y + 1) // 8

    def at_band(b):
        return {"band": b, "tile": tile}

    def at_tile(t):
        return {"band": band, "tile": lax.rem(t + TILE, TILE)}

    barrier = pltpu.get_barrier_semaphore()
    peers = [at_band(lax.rem(band + o, BAND)) for o in range(1, BAND)]
    other_z = tile + 1 - 2 * z
    above, below = tile + 2 - 16 * last, tile - 2 + 16 * first
    peers += [at_tile(t) for t in (tile + 16, tile - 16, tile + 32)]
    peers += [at_tile(t) for t in (tile + 2, tile - 2, above, below)]
    for peer in peers:
        pl.semaphore_signal(barrier, inc=1, device_id=peer, device_id_type=MESH)

    @pl.when(jnp.logical_not(home))
    def _():
        for b in range(BAND):
            peer = {"band": b, "tile": other_z}
            pl.semaphore_signal(barrier, inc=1, device_id=peer, device_id_type=MESH)

    wave_copy = pltpu.make_async_copy(wave_hbm, wave, in_sem.at[0])
    fwd_copy = pltpu.make_async_copy(fwd_hbm, fwd, in_sem.at[1])
    widths_copy = pltpu.make_async_copy(widths_hbm, widths, in_sem.at[2])
    kt_copy = pltpu.make_async_copy(inv_all.at[group], kt, in_sem.at[3])
    select_copy = pltpu.make_async_copy(select_hbm, select, in_sem.at[4])
    for copy in (wave_copy, fwd_copy, widths_copy, kt_copy, select_copy):
        copy.start()
    wave_copy.wait()
    fwd_copy.wait()
    widths_copy.wait()

    nt = (((1,), (1,)), ((), ()))
    samples = jnp.concatenate([wave[:, s, :] for s in range(SEGL)], axis=0)
    spectra = lax.dot_general(fwd[...], samples, nt, preferred_element_type=f32).astype(bf16)
    values = spectra.astype(f32)
    squares = values * values
    sq_hi = squares.astype(bf16)
    sq_lo = (squares - sq_hi.astype(f32)).astype(bf16)
    offsets = []
    total = widths[0] * 0
    for b in range(BAND):
        offsets.append(total)
        total = total + widths[b]

    def member(rows, bins):
        low = jnp.zeros(rows.shape, jnp.int32)
        size = jnp.zeros(rows.shape, jnp.int32)
        for b in range(BAND):
            low = jnp.where(rows == b, offsets[b], low)
            size = jnp.where(rows == b, widths[b], size)
        return jnp.where((bins >= low) & (bins < low + size), 1.0, 0.0).astype(f32)

    shape = (BAND, BINGROUPS * ROWS)
    is_in = member(
        lax.broadcasted_iota(jnp.int32, shape, 0), lax.broadcasted_iota(jnp.int32, shape, 1) // 2
    ).astype(bf16)
    part = jnp.dot(is_in, sq_hi, preferred_element_type=f32)
    part = part + jnp.dot(is_in, sq_lo, preferred_element_type=f32)
    part_hi = part.astype(bf16).astype(f32)
    energies = jnp.concatenate([part_hi, part - part_hi], axis=0).astype(bf16)
    for b in range(BINGROUPS):
        sb[b, :ROWS] = spectra[b * ROWS : (b + 1) * ROWS]
        sb[b, ROWS:] = energies
    rb[0, 0] = sb[group]

    pl.semaphore_wait(barrier, len(peers) + BINGROUPS)

    exchange = []

    def share(n, to, tile_to, which, sems):
        o = lax.rem(to - band + BAND, BAND)
        copy = pltpu.make_async_remote_copy(
            src_ref=sb.at[lax.rem(to, BINGROUPS)],
            dst_ref=rb.at[which, o],
            send_sem=a_send.at[n],
            recv_sem=sems.at[o],
            device_id={"band": to, "tile": tile_to},
            device_id_type=MESH,
        )
        if which:
            copy.start()
        else:
            pl.when(to != band)(copy.start)
        exchange.append((to, which, copy))

    for j in range(BINGROUPS):
        share(j, 4 * z + j, tile, 0, a_recv)
        share(4 + j, 4 * z + j, other_z, 1, o_recv)
    for j in range(BINGROUPS):
        share(8 + j, 4 - 4 * z + j, tile, 0, a_recv)

    def collect(which):
        for o in range(1 - which, BAND):
            pltpu.make_async_remote_copy(
                src_ref=sb.at[0],
                dst_ref=rb.at[which, o],
                send_sem=a_send.at[0],
                recv_sem=(o_recv if which else a_recv).at[o],
                device_id={"band": band, "tile": other_z},
                device_id_type=MESH,
            ).wait_recv()

    lane = lax.broadcasted_iota(jnp.int32, (CH, 128), 1)

    def whiten(which):
        energy = jnp.zeros((BAND, 128), f32)
        for o in range(BAND):
            tail = rb[which, o, ROWS:].astype(f32)
            energy = energy + tail[:BAND] + tail[BAND:]
        energy = energy + pltpu.roll(energy, 64, 1)
        energy = energy + pltpu.roll(energy, 32, 1)
        row8 = lax.broadcasted_iota(jnp.int32, (BAND, 128), 0)
        width8 = jnp.ones((BAND, 128), f32)
        for b in range(BAND):
            width8 = jnp.where(row8 == b, widths[b].astype(f32), width8)
        gain = lax.rsqrt(energy / (SEG * width8) + EPS)
        bins = group * QN + lax.broadcasted_iota(jnp.int32, (ROWS, 128), 0) // 2
        gains = jnp.zeros((ROWS, 128), f32)
        for b in range(BAND):
            inside = (bins >= offsets[b]) & (bins < offsets[b] + widths[b])
            gains = jnp.where(inside, gain[b : b + 1, :], gains)
        white = [
            (rb[which, o, :ROWS].astype(f32) * gains).astype(bf16).astype(f32) for o in range(BAND)
        ]
        tiles = []
        for pair in range(GROUPS // 2):
            stack = jnp.concatenate(
                [
                    white[o][(2 * pair + h) * 8 : (2 * pair + h + 1) * 8]
                    for h in range(2)
                    for o in range(BAND)
                ],
                axis=0,
            )
            flipped = jnp.transpose(stack)
            rolled = pltpu.roll(flipped, 64, 1)
            seg = [flipped[s * CH : (s + 1) * CH] for s in range(SEGL)]
            seg_r = [rolled[s * CH : (s + 1) * CH] for s in range(SEGL)]
            for low, high in ((seg, seg_r), (seg_r, seg)):
                tiles.append([jnp.where(lane < 64, low[2 * v], high[2 * v + 1]) for v in range(2)])
        return tiles

    pl.when(home)(lambda: collect(0))
    pl.when(jnp.logical_not(home))(lambda: collect(1))
    for n, halves in enumerate(whiten(lax.rem(z + side, 2))):
        for v in range(2):
            first_lane = n % (GROUPS // 2) * 256 + v * 128
            g[n // (GROUPS // 2), :CH, first_lane : first_lane + 128] = halves[v].astype(bf16)

    def slot(r, h, instead=None, when=None):
        row = POS[r] * CH
        if instead is not None:
            row = pl.multiple_of(row + when * (POS[instead] - POS[r]) * CH, CH)
        return g.at[h, pl.ds(row, CH)]

    copies = {}

    def describe(name, src, dst, to):
        n = len(copies)
        copies[name] = pltpu.make_async_remote_copy(
            src_ref=src,
            dst_ref=dst,
            send_sem=g_send.at[n],
            recv_sem=g_recv.at[n],
            device_id=at_tile(to),
            device_id_type=MESH,
        )

    for h in range(2):
        describe((8, h), slot(0, h), slot(8, h), tile + 16)
        describe((16, h), slot(0, h), slot(16, h), tile + 32)
        for k in range(1, 5):
            describe((k, h), slot(k - 1, h, 7 + k, last), slot(k, h), above)
            if k < 4:
                describe((8 - k, h), slot(9 - k, h), slot(8 - k, h), tile - 2)
            if 1 < k < 4:
                describe((8 + k, h), slot(7 + k, h), slot(8 + k, h), tile + 2)
            if k > 1:
                describe((16 - k, h), slot(17 - k, h, 9 - k, first), slot(16 - k, h), below)
        describe((9, h), slot(1, h), slot(9, h), tile + 16)
        describe((15, h), slot(7, h), slot(15, h), tile + 16)

    def arrive(r, h):
        def start(other):
            copies[(other, h)].start()

        if r:
            copies[(r, h)].wait_recv()
        if r == 0:
            pl.when(last == 0)(lambda: start(1))
            start(8)
        elif r == 8:
            pl.when(last == 1)(lambda: start(1))
            start(7)
        elif r < 4:
            pl.when(last == 0)(lambda: start(r + 1))
            if r == 1:
                start(9)
        elif 4 < r < 8:
            if r > 5:
                start(r - 1)
            pl.when(first == 1)(lambda: start(r + 7))
            if r == 7:
                start(15)
        elif 8 < r < 12:
            pl.when(last == 1)(lambda: start(r - 7))
            if r < 11:
                start(r + 1)
        elif 12 < r < 16:
            pl.when(first == 0)(lambda: start(r - 1))

    arrive(0, 0)
    arrive(0, 1)
    for h in range(2):
        copies[(16, h)].start()

    even = lax.rem(lane, 2) == 0
    bin4 = lax.rem(lane // 2, 4)
    pl.when(jnp.logical_not(home))(lambda: collect(0))
    for n, halves in enumerate(whiten(0)):
        for v in range(2):
            own = halves[v]
            alt = jnp.where(even, pltpu.roll(own, 127, 1), -pltpu.roll(own, 1, 1))
            for q in range(4):
                kept = [jnp.where(bin4 == q, values, 0.0) for values in (own, alt)]
                for quarter in range(4):
                    rows = [values[quarter * 8 : quarter * 8 + 8] for values in kept]
                    row = quarter * 64 + q * 16
                    wt[n, row : row + 16, v * 128 : (v + 1) * 128] = jnp.concatenate(rows, axis=0).astype(bf16)

    wide = lax.broadcasted_iota(jnp.int32, (PART, 128), 1)

    def compute(k):
        start, blocks = CHUNKS[k]
        rows = PACKED[blocks]
        for n in range(GROUPS):
            low = n % (GROUPS // 2) * 256
            block = g[n // (GROUPS // 2), start * CH : (start + blocks) * CH, low : low + 256]
            block = jnp.concatenate([block] * (4 // blocks), axis=0)
            cross = lax.dot_general(wt[n], block, nt, preferred_element_type=f32).astype(bf16)
            for quarter in range(4):
                lanes = slice(quarter * 128, (quarter + 1) * 128)
                ct[n * 64 : (n + 1) * 64, lanes] = cross[quarter * 64 : (quarter + 1) * 64]
        lags = jnp.dot(kt[...], ct[...], preferred_element_type=f32) * SCALE
        for quarter in range(4):
            for b2 in range(2):
                share = lags[b2 * PART : (b2 + 1) * PART, quarter * 128 : (quarter + 1) * 128]
                if blocks < 4:
                    copies_of = 4 // blocks
                    step = (PART - rows) // (copies_of - 1)
                    packed = share[:rows]
                    for i in range(1, copies_of):
                        here = wide[:rows] // (32 * blocks) == i
                        packed = jnp.where(here, share[i * step : i * step + rows], packed)
                    share = packed
                parts[k, b2, quarter, :rows] = share.astype(bf16)

    def place(k, region, share):
        start, blocks = CHUNKS[k]
        rows = PACKED[blocks]
        if blocks < 4:
            copies_of = 4 // blocks
            step = (PART - rows) // (copies_of - 1)
            pieces = [share]
            for i in range(1, copies_of):
                pieces.append(pltpu.roll(share, 128 - 32 * blocks * i, 1)[rows - step :])
            share = jnp.concatenate(pieces, axis=0)
        turned = lax.dot_general(
            share.astype(bf16), select[...], (((0,), (0,)), ((), ())), preferred_element_type=f32
        ).astype(bf16)
        for b in range(blocks):
            for i4 in range(4):
                lags = turned[b * CH : (b + 1) * CH, i4 * 128 : i4 * 128 + LAGS]
                out[region * 17 + start + b, i4] = lags

    adding = {}

    def send(name, n, k, src, dst, to):
        copy = pltpu.make_async_remote_copy(
            src_ref=src,
            dst_ref=dst,
            send_sem=r_send.at[k * 4 + n],
            recv_sem=r_recv.at[k * 4 + n],
            device_id=at_band(to),
            device_id_type=MESH,
        )
        copy.start()
        adding[(name, k)] = copy

    odd = lax.rem(zh, 2)
    mate, beyond, far = zh + 1 - 2 * odd, lax.rem(zh + 2 * odd + 3, 4), lax.rem(zh + 2, 4)
    to_sibling, to_mate, to_beyond = 2 * zh + 1 - core, 2 * mate + core, 2 * beyond + core
    to_far = 2 * far + core

    def r0(k):
        compute(k)
        rows = pl.ds(0, PACKED[CHUNKS[k][1]])
        send("sib", 0, k, parts.at[k, 1 - core, :, rows], theirs.at[k, :, rows], to_sibling)

    def r1(k):
        rows = PACKED[CHUNKS[k][1]]
        adding[("sib", k)].wait_recv()

        def both(n):
            return parts[k, core, n, :rows].astype(f32) + theirs[k, n, :rows].astype(f32)

        cut = pl.ds(0, rows)
        if k in DIRECT:
            pair_out[k, 1, :rows] = both(far).astype(bf16)
            send("far", 3, k, pair_out.at[k, 1, cut], final.at[k, 1, cut], to_far)
            pair_out[k, 0, :rows] = both(mate).astype(bf16)
            send("pair", 1, k, pair_out.at[k, 0, cut], pair_in.at[k, 0, cut], to_mate)
            outer[k, :rows] = both(beyond).astype(bf16)
            send("out", 2, k, outer.at[k, cut], final.at[k, 0, cut], to_beyond)
        else:
            pair_out[k, 0, :rows] = both(mate).astype(bf16)
            pair_out[k, 1, :rows] = both(far).astype(bf16)
            send("pair", 1, k, pair_out.at[k, :, cut], pair_in.at[k, :, cut], to_mate)
            outer[k, :rows] = both(beyond).astype(bf16)
        mine[k, :rows] = both(zh).astype(bf16)

    def r2(k):
        rows = PACKED[CHUNKS[k][1]]
        adding[("pair", k)].wait_recv()
        if k not in DIRECT:
            passed = outer[k, :rows].astype(f32) + pair_in[k, 1, :rows].astype(f32)
            outer[k, :rows] = passed.astype(bf16)
            send("out", 2, k, outer.at[k, pl.ds(0, rows)], final.at[k, 0, pl.ds(0, rows)], to_beyond)
        place(k, 0, mine[k, :rows].astype(f32) + pair_in[k, 0, :rows].astype(f32))

    def r3(k):
        rows = PACKED[CHUNKS[k][1]]
        adding[("out", k)].wait_recv()
        whole = final[k, 0, :rows].astype(f32)
        if k in DIRECT:
            adding[("far", k)].wait_recv()
            whole = whole + final[k, 1, :rows].astype(f32)
        place(k, 1, whole)

    kt_copy.wait()
    select_copy.wait()
    stages = {"c": r0, "s": r1, "m": r2, "f": r3}
    arrive(8, 0)

    @pl.when(first == 1)
    def _():
        arrive(8, 1)
        arrive(1, 0)

    @pl.when(first == 0)
    def _():
        arrive(1, 0)
        arrive(8, 1)

    for step in STEPS:
        if step[0] in stages:
            stages[step[0]](int(step[1:]))
        else:
            arrive(int(step[:-1]), "ab".index(step[-1]))

    for to, which, copy in exchange:
        if which:
            copy.wait_send()
        else:
            pl.when(to != band)(copy.wait_send)
    for copy in copies.values():
        copy.wait_send()
    for copy in adding.values():
        copy.wait_send()


def _place_kernel(table, place, turned, out):
    tile = lax.axis_index("tile")
    side = lax.axis_index("band") // 4

    def step(s, carry):
        partner = table[0, s]
        behind = lax.rem(tile // 2 - partner // 2 + TILE // 2, TILE // 2)
        out[s] = turned[place[behind] + lax.rem(partner + side, 2) * 17]
        return carry

    lax.fori_loop(0, out.shape[0], step, 0)


def body(waveforms, band_widths, pair_table):
    slots = pair_table.shape[1]
    bf16 = jnp.bfloat16
    scratch = [
        pltpu.SMEM((BAND,), jnp.int32),
        pltpu.VMEM(waveforms.shape, bf16),
        pltpu.VMEM((BINGROUPS * ROWS, SAMPLES), bf16),
        pltpu.VMEM((BINGROUPS, MSG, 128), bf16),
        pltpu.VMEM((2, BAND, MSG, 128), bf16),
        pltpu.VMEM((2, 17 * CH, WIDE // 2), bf16),
        pltpu.VMEM((GROUPS, 256, 256), bf16),
        pltpu.VMEM((2 * PART, GROUPS * 64), bf16),
        pltpu.VMEM((GROUPS * 64, 512), bf16),
        pltpu.VMEM((len(CHUNKS), 2, 4, PART, 128), bf16),
        pltpu.VMEM((len(CHUNKS), 4, PART, 128), bf16),
        pltpu.VMEM((len(CHUNKS), PART, 128), bf16),
        pltpu.VMEM((len(CHUNKS), 2, PART, 128), bf16),
        pltpu.VMEM((len(CHUNKS), 2, PART, 128), bf16),
        pltpu.VMEM((len(CHUNKS), PART, 128), bf16),
        pltpu.VMEM((len(CHUNKS), 2, PART, 128), bf16),
        pltpu.VMEM((PART, 512), bf16),
    ]
    dma = pltpu.SemaphoreType.DMA
    scratch += [
        dma((5,)),
        dma((12,)),
        dma((BAND,)),
        dma((BAND,)),
        dma((32,)),
        dma((32,)),
        dma((4 * len(CHUNKS),)),
        dma((4 * len(CHUNKS),)),
    ]
    vmem = pl.BlockSpec(memory_space=pltpu.VMEM)
    smem = pl.BlockSpec(memory_space=pltpu.SMEM)
    summed = pl.pallas_call(
        _main_kernel,
        out_shape=jax.ShapeDtypeStruct((34, 4, CH, LAGS), bf16),
        in_specs=[pl.BlockSpec(memory_space=pl.ANY)] * 5,
        out_specs=vmem,
        scratch_shapes=scratch,
        compiler_params=pltpu.CompilerParams(
            collective_id=0, has_side_effects=True, vmem_limit_bytes=60 * 1024 * 1024
        ),
        name="correlate",
    )(
        band_widths,
        waveforms,
        jnp.asarray(_forward_const()),
        jnp.asarray(_inverse_const()),
        jnp.asarray(_select_const()),
    )
    place = np.zeros((TILE // 2,), np.int32)
    for r, i in POS.items():
        place[r] = i
    placed = pl.pallas_call(
        _place_kernel,
        out_shape=jax.ShapeDtypeStruct((slots, 4, CH, LAGS), bf16),
        in_specs=[smem, smem, vmem],
        out_specs=vmem,
        name="place",
    )(pair_table, jnp.asarray(place), summed)
    return placed[None]


def solution(mesh):
    placed = (P("tile", "band", None), P(), P("tile", None))
    return jax.shard_map(
        body,
        mesh=mesh,
        in_specs=placed,
        out_specs=P("tile", None, "band", None, None),
        check_vma=False,
    )
```

```python
import functools
import math

import jax
import jax.numpy as jnp
import ml_dtypes
import numpy as np
from jax import lax
from jax.experimental import pallas as pl
from jax.experimental.pallas import tpu as pltpu
from jax.sharding import PartitionSpec as P

BINS = 180
FIRST = 20
LAGS = 51
SAMPLES = 500
EPS = 1e-05

BAND = 8
TILE = 64
CH = 32
SEG = 32
SEGL = 4
QN = 48
BINGROUPS = 4
GROUPS = QN // 4
ROWS = 2 * QN
MSG = ROWS + 16
WIDE = QN * 64
PART = 208
SCALE = 1.0 / math.sqrt(SEG * BINS)
MESH = pl.DeviceIdType.MESH

ORDER = [0, 8, 16, 1, 7, 9, 15, 2, 6, 10, 14, 3, 5, 11, 13, 4, 12]
POS = {r: i for i, r in enumerate(ORDER)}
CHUNKS = [(0, 4), (4, 4), (8, 4), (12, 2), (14, 2), (16, 1)]
PACKED = {4: PART, 2: 112, 1: 64}
DIRECT = (3, 4, 5)
STEPS = [
    "1b", "7a", "9a", "16a", "16b", "7b", "9b", "c0",
    "2a", "15a", "s0", "2b", "15b", "10a", "10b", "6a", "c1",
    "3a", "s1", "6b", "14a", "3b", "14b", "c2",
    "5a", "m0", "11b", "11a", "5b", "s2", "c3",
    "13a", "4a", "m1", "s3", "4b", "13b", "c4",
    "s4", "12a", "m2", "12b", "c5",
    "m3", "s5", "f0", "f1", "f2", "f3", "m4", "f4", "m5", "f5",
]


def _forward_const():
    n = np.arange(SAMPLES)
    table = np.zeros((BINGROUPS * QN, 2, SAMPLES), np.float32)
    for k in range(BINS):
        angle = ((n * (FIRST + k)) % SAMPLES) * (2.0 * math.pi / SAMPLES)
        table[k, 0] = np.cos(angle)
        table[k, 1] = -np.sin(angle)
    return table.reshape(BINGROUPS * ROWS, SAMPLES).astype(ml_dtypes.bfloat16)


def _inverse_const():
    tau = np.arange(LAGS) - LAGS // 2
    table = np.zeros((BINGROUPS * QN, 2, LAGS), np.float32)
    for k in range(BINS):
        angle = (((FIRST + k) * tau) % SAMPLES) * (2.0 * math.pi / SAMPLES)
        table[k, 0] = np.cos(angle)
        table[k, 1] = -np.sin(angle)
    table = table.reshape(BINGROUPS, GROUPS, 4, 2, LAGS)
    out = np.zeros((BINGROUPS, 2, PART, GROUPS, 4, 2, 8), np.float32)
    for b2 in range(2):
        for i4 in range(4):
            rows = np.moveaxis(table, -1, 1)
            out[:, b2, i4 * LAGS : (i4 + 1) * LAGS, :, :, :, b2 * 4 + i4] = rows
    return out.reshape(BINGROUPS, 2 * PART, GROUPS * 64).astype(ml_dtypes.bfloat16)


def _select_const():
    out = np.zeros((PART, 512), np.float32)
    for i4 in range(4):
        for lag in range(LAGS):
            out[i4 * LAGS + lag, i4 * 128 + lag] = 1.0
    return out.astype(ml_dtypes.bfloat16)


def _main_kernel(widths_hbm, wave_hbm, fwd_hbm, inv_all, select_hbm, out, *scratch):
    widths, wave, fwd, sb, rb, g, wt, kt, ct = scratch[:9]
    parts, theirs, mine, pair_out, pair_in, outer, final, select = scratch[9:17]
    (in_sem, a_send, a_recv, o_recv, g_send, g_recv, r_send, r_recv) = scratch[17:]
    f32, bf16 = jnp.float32, jnp.bfloat16

    band = lax.axis_index("band")
    tile = lax.axis_index("tile")
    core = lax.rem(band, 2)
    zh = band // 2
    z = lax.rem(tile, 2)
    side = band // 4
    group = lax.rem(band, BINGROUPS)
    home = z == side
    y = lax.rem(tile // 2, 8)
    first = (7 - y) // 7
    last = (y + 1) // 8

    def at_band(b):
        return {"band": b, "tile": tile}

    def at_tile(t):
        return {"band": band, "tile": lax.rem(t + TILE, TILE)}

    barrier = pltpu.get_barrier_semaphore()
    peers = [at_band(lax.rem(band + o, BAND)) for o in range(1, BAND)]
    other_z = tile + 1 - 2 * z
    above, below = tile + 2 - 16 * last, tile - 2 + 16 * first
    peers += [at_tile(t) for t in (tile + 16, tile - 16, tile + 32)]
    peers += [at_tile(t) for t in (tile + 2, tile - 2, above, below)]
    for peer in peers:
        pl.semaphore_signal(barrier, inc=1, device_id=peer, device_id_type=MESH)

    @pl.when(jnp.logical_not(home))
    def _():
        for b in range(BAND):
            peer = {"band": b, "tile": other_z}
            pl.semaphore_signal(barrier, inc=1, device_id=peer, device_id_type=MESH)

    wave_copy = pltpu.make_async_copy(wave_hbm, wave, in_sem.at[0])
    fwd_copy = pltpu.make_async_copy(fwd_hbm, fwd, in_sem.at[1])
    widths_copy = pltpu.make_async_copy(widths_hbm, widths, in_sem.at[2])
    kt_copy = pltpu.make_async_copy(inv_all.at[group], kt, in_sem.at[3])
    select_copy = pltpu.make_async_copy(select_hbm, select, in_sem.at[4])
    for copy in (wave_copy, fwd_copy, widths_copy, kt_copy, select_copy):
        copy.start()
    wave_copy.wait()
    fwd_copy.wait()
    widths_copy.wait()

    nt = (((1,), (1,)), ((), ()))
    samples = jnp.concatenate([wave[:, s, :] for s in range(SEGL)], axis=0)
    spectra = lax.dot_general(fwd[...], samples, nt, preferred_element_type=f32).astype(bf16)
    values = spectra.astype(f32)
    squares = values * values
    sq_hi = squares.astype(bf16)
    sq_lo = (squares - sq_hi.astype(f32)).astype(bf16)
    offsets = []
    total = widths[0] * 0
    for b in range(BAND):
        offsets.append(total)
        total = total + widths[b]

    def member(rows, bins):
        low = jnp.zeros(rows.shape, jnp.int32)
        size = jnp.zeros(rows.shape, jnp.int32)
        for b in range(BAND):
            low = jnp.where(rows == b, offsets[b], low)
            size = jnp.where(rows == b, widths[b], size)
        return jnp.where((bins >= low) & (bins < low + size), 1.0, 0.0).astype(f32)

    shape = (BAND, BINGROUPS * ROWS)
    is_in = member(
        lax.broadcasted_iota(jnp.int32, shape, 0), lax.broadcasted_iota(jnp.int32, shape, 1) // 2
    ).astype(bf16)
    part = jnp.dot(is_in, sq_hi, preferred_element_type=f32)
    part = part + jnp.dot(is_in, sq_lo, preferred_element_type=f32)
    part_hi = part.astype(bf16).astype(f32)
    energies = jnp.concatenate([part_hi, part - part_hi], axis=0).astype(bf16)
    for b in range(BINGROUPS):
        sb[b, :ROWS] = spectra[b * ROWS : (b + 1) * ROWS]
        sb[b, ROWS:] = energies
    rb[0, 0] = sb[group]

    pl.semaphore_wait(barrier, len(peers) + BINGROUPS)

    exchange = []

    def share(n, to, tile_to, which, sems):
        o = lax.rem(to - band + BAND, BAND)
        copy = pltpu.make_async_remote_copy(
            src_ref=sb.at[lax.rem(to, BINGROUPS)],
            dst_ref=rb.at[which, o],
            send_sem=a_send.at[n],
            recv_sem=sems.at[o],
            device_id={"band": to, "tile": tile_to},
            device_id_type=MESH,
        )
        if which:
            copy.start()
        else:
            pl.when(to != band)(copy.start)
        exchange.append((to, which, copy))

    for j in range(BINGROUPS):
        share(j, 4 * z + j, tile, 0, a_recv)
        share(4 + j, 4 * z + j, other_z, 1, o_recv)
    for j in range(BINGROUPS):
        share(8 + j, 4 - 4 * z + j, tile, 0, a_recv)

    def collect(which):
        for o in range(1 - which, BAND):
            pltpu.make_async_remote_copy(
                src_ref=sb.at[0],
                dst_ref=rb.at[which, o],
                send_sem=a_send.at[0],
                recv_sem=(o_recv if which else a_recv).at[o],
                device_id={"band": band, "tile": other_z},
                device_id_type=MESH,
            ).wait_recv()

    lane = lax.broadcasted_iota(jnp.int32, (CH, 128), 1)

    def whiten(which):
        energy = jnp.zeros((BAND, 128), f32)
        for o in range(BAND):
            tail = rb[which, o, ROWS:].astype(f32)
            energy = energy + tail[:BAND] + tail[BAND:]
        energy = energy + pltpu.roll(energy, 64, 1)
        energy = energy + pltpu.roll(energy, 32, 1)
        row8 = lax.broadcasted_iota(jnp.int32, (BAND, 128), 0)
        width8 = jnp.ones((BAND, 128), f32)
        for b in range(BAND):
            width8 = jnp.where(row8 == b, widths[b].astype(f32), width8)
        gain = lax.rsqrt(energy / (SEG * width8) + EPS)
        bins = group * QN + lax.broadcasted_iota(jnp.int32, (ROWS, 128), 0) // 2
        gains = jnp.zeros((ROWS, 128), f32)
        for b in range(BAND):
            inside = (bins >= offsets[b]) & (bins < offsets[b] + widths[b])
            gains = jnp.where(inside, gain[b : b + 1, :], gains)
        white = [
            (rb[which, o, :ROWS].astype(f32) * gains).astype(bf16).astype(f32) for o in range(BAND)
        ]
        tiles = []
        for pair in range(GROUPS // 2):
            stack = jnp.concatenate(
                [
                    white[o][(2 * pair + h) * 8 : (2 * pair + h + 1) * 8]
                    for h in range(2)
                    for o in range(BAND)
                ],
                axis=0,
            )
            flipped = jnp.transpose(stack)
            rolled = pltpu.roll(flipped, 64, 1)
            seg = [flipped[s * CH : (s + 1) * CH] for s in range(SEGL)]
            seg_r = [rolled[s * CH : (s + 1) * CH] for s in range(SEGL)]
            for low, high in ((seg, seg_r), (seg_r, seg)):
                tiles.append([jnp.where(lane < 64, low[2 * v], high[2 * v + 1]) for v in range(2)])
        return tiles

    pl.when(home)(lambda: collect(0))
    pl.when(jnp.logical_not(home))(lambda: collect(1))
    for n, halves in enumerate(whiten(lax.rem(z + side, 2))):
        for v in range(2):
            first_lane = n % (GROUPS // 2) * 256 + v * 128
            g[n // (GROUPS // 2), :CH, first_lane : first_lane + 128] = halves[v].astype(bf16)

    def slot(r, h, instead=None, when=None):
        row = POS[r] * CH
        if instead is not None:
            row = pl.multiple_of(row + when * (POS[instead] - POS[r]) * CH, CH)
        return g.at[h, pl.ds(row, CH)]

    copies = {}

    def describe(name, src, dst, to):
        n = len(copies)
        copies[name] = pltpu.make_async_remote_copy(
            src_ref=src,
            dst_ref=dst,
            send_sem=g_send.at[n],
            recv_sem=g_recv.at[n],
            device_id=at_tile(to),
            device_id_type=MESH,
        )

    for h in range(2):
        describe((8, h), slot(0, h), slot(8, h), tile + 16)
        describe((16, h), slot(0, h), slot(16, h), tile + 32)
        for k in range(1, 5):
            describe((k, h), slot(k - 1, h, 7 + k, last), slot(k, h), above)
            if k < 4:
                describe((8 - k, h), slot(9 - k, h), slot(8 - k, h), tile - 2)
            if 1 < k < 4:
                describe((8 + k, h), slot(7 + k, h), slot(8 + k, h), tile + 2)
            if k > 1:
                describe((16 - k, h), slot(17 - k, h, 9 - k, first), slot(16 - k, h), below)
        describe((9, h), slot(1, h), slot(9, h), tile + 16)
        describe((15, h), slot(7, h), slot(15, h), tile + 16)

    def arrive(r, h):
        def start(other):
            copies[(other, h)].start()

        if r:
            copies[(r, h)].wait_recv()
        if r == 0:
            pl.when(last == 0)(lambda: start(1))
            start(8)
        elif r == 8:
            pl.when(last == 1)(lambda: start(1))
            start(7)
        elif r < 4:
            pl.when(last == 0)(lambda: start(r + 1))
            if r == 1:
                start(9)
        elif 4 < r < 8:
            if r > 5:
                start(r - 1)
            pl.when(first == 1)(lambda: start(r + 7))
            if r == 7:
                start(15)
        elif 8 < r < 12:
            pl.when(last == 1)(lambda: start(r - 7))
            if r < 11:
                start(r + 1)
        elif 12 < r < 16:
            pl.when(first == 0)(lambda: start(r - 1))

    arrive(0, 0)
    arrive(0, 1)
    for h in range(2):
        copies[(16, h)].start()

    even = lax.rem(lane, 2) == 0
    bin4 = lax.rem(lane // 2, 4)
    pl.when(jnp.logical_not(home))(lambda: collect(0))
    for n, halves in enumerate(whiten(0)):
        for v in range(2):
            own = halves[v]
            alt = jnp.where(even, pltpu.roll(own, 127, 1), -pltpu.roll(own, 1, 1))
            for q in range(4):
                kept = [jnp.where(bin4 == q, values, 0.0) for values in (own, alt)]
                for quarter in range(4):
                    rows = [values[quarter * 8 : quarter * 8 + 8] for values in kept]
                    row = quarter * 64 + q * 16
                    wt[n, row : row + 16, v * 128 : (v + 1) * 128] = jnp.concatenate(rows, axis=0).astype(bf16)

    wide = lax.broadcasted_iota(jnp.int32, (PART, 128), 1)

    def compute(k):
        start, blocks = CHUNKS[k]
        rows = PACKED[blocks]
        for n in range(GROUPS):
            low = n % (GROUPS // 2) * 256
            block = g[n // (GROUPS // 2), start * CH : (start + blocks) * CH, low : low + 256]
            block = jnp.concatenate([block] * (4 // blocks), axis=0)
            cross = lax.dot_general(wt[n], block, nt, preferred_element_type=f32).astype(bf16)
            for quarter in range(4):
                lanes = slice(quarter * 128, (quarter + 1) * 128)
                ct[n * 64 : (n + 1) * 64, lanes] = cross[quarter * 64 : (quarter + 1) * 64]
        lags = jnp.dot(kt[...], ct[...], preferred_element_type=f32) * SCALE
        for quarter in range(4):
            for b2 in range(2):
                share = lags[b2 * PART : (b2 + 1) * PART, quarter * 128 : (quarter + 1) * 128]
                if blocks < 4:
                    copies_of = 4 // blocks
                    step = (PART - rows) // (copies_of - 1)
                    packed = share[:rows]
                    for i in range(1, copies_of):
                        here = wide[:rows] // (32 * blocks) == i
                        packed = jnp.where(here, share[i * step : i * step + rows], packed)
                    share = packed
                parts[k, b2, quarter, :rows] = share.astype(bf16)

    def place(k, region, share):
        start, blocks = CHUNKS[k]
        rows = PACKED[blocks]
        if blocks < 4:
            copies_of = 4 // blocks
            step = (PART - rows) // (copies_of - 1)
            pieces = [share]
            for i in range(1, copies_of):
                pieces.append(pltpu.roll(share, 128 - 32 * blocks * i, 1)[rows - step :])
            share = jnp.concatenate(pieces, axis=0)
        turned = lax.dot_general(
            share.astype(bf16), select[...], (((0,), (0,)), ((), ())), preferred_element_type=f32
        ).astype(bf16)
        for b in range(blocks):
            for i4 in range(4):
                lags = turned[b * CH : (b + 1) * CH, i4 * 128 : i4 * 128 + LAGS]
                out[region * 17 + start + b, i4] = lags

    adding = {}

    def send(name, n, k, src, dst, to):
        copy = pltpu.make_async_remote_copy(
            src_ref=src,
            dst_ref=dst,
            send_sem=r_send.at[k * 4 + n],
            recv_sem=r_recv.at[k * 4 + n],
            device_id=at_band(to),
            device_id_type=MESH,
        )
        copy.start()
        adding[(name, k)] = copy

    odd = lax.rem(zh, 2)
    mate, beyond, far = zh + 1 - 2 * odd, lax.rem(zh + 2 * odd + 3, 4), lax.rem(zh + 2, 4)
    to_sibling, to_mate, to_beyond = 2 * zh + 1 - core, 2 * mate + core, 2 * beyond + core
    to_far = 2 * far + core

    def r0(k):
        compute(k)
        rows = pl.ds(0, PACKED[CHUNKS[k][1]])
        send("sib", 0, k, parts.at[k, 1 - core, :, rows], theirs.at[k, :, rows], to_sibling)

    def r1(k):
        rows = PACKED[CHUNKS[k][1]]
        adding[("sib", k)].wait_recv()

        def both(n):
            return parts[k, core, n, :rows].astype(f32) + theirs[k, n, :rows].astype(f32)

        cut = pl.ds(0, rows)
        if k in DIRECT:
            pair_out[k, 1, :rows] = both(far).astype(bf16)
            send("far", 3, k, pair_out.at[k, 1, cut], final.at[k, 1, cut], to_far)
            pair_out[k, 0, :rows] = both(mate).astype(bf16)
            send("pair", 1, k, pair_out.at[k, 0, cut], pair_in.at[k, 0, cut], to_mate)
            outer[k, :rows] = both(beyond).astype(bf16)
            send("out", 2, k, outer.at[k, cut], final.at[k, 0, cut], to_beyond)
        else:
            pair_out[k, 0, :rows] = both(mate).astype(bf16)
            pair_out[k, 1, :rows] = both(far).astype(bf16)
            send("pair", 1, k, pair_out.at[k, :, cut], pair_in.at[k, :, cut], to_mate)
            outer[k, :rows] = both(beyond).astype(bf16)
        mine[k, :rows] = both(zh).astype(bf16)

    def r2(k):
        rows = PACKED[CHUNKS[k][1]]
        adding[("pair", k)].wait_recv()
        if k not in DIRECT:
            passed = outer[k, :rows].astype(f32) + pair_in[k, 1, :rows].astype(f32)
            outer[k, :rows] = passed.astype(bf16)
            send("out", 2, k, outer.at[k, pl.ds(0, rows)], final.at[k, 0, pl.ds(0, rows)], to_beyond)
        place(k, 0, mine[k, :rows].astype(f32) + pair_in[k, 0, :rows].astype(f32))

    def r3(k):
        rows = PACKED[CHUNKS[k][1]]
        adding[("out", k)].wait_recv()
        whole = final[k, 0, :rows].astype(f32)
        if k in DIRECT:
            adding[("far", k)].wait_recv()
            whole = whole + final[k, 1, :rows].astype(f32)
        place(k, 1, whole)

    kt_copy.wait()
    select_copy.wait()
    stages = {"c": r0, "s": r1, "m": r2, "f": r3}
    arrive(8, 0)

    @pl.when(first == 1)
    def _():
        arrive(8, 1)
        arrive(1, 0)

    @pl.when(first == 0)
    def _():
        arrive(1, 0)
        arrive(8, 1)

    for step in STEPS:
        if step[0] in stages:
            stages[step[0]](int(step[1:]))
        else:
            arrive(int(step[:-1]), "ab".index(step[-1]))

    for to, which, copy in exchange:
        if which:
            copy.wait_send()
        else:
            pl.when(to != band)(copy.wait_send)
    for copy in copies.values():
        copy.wait_send()
    for copy in adding.values():
        copy.wait_send()


def _place_kernel(table, place, turned, out):
    tile = lax.axis_index("tile")
    side = lax.axis_index("band") // 4

    def step(s, carry):
        partner = table[0, s]
        behind = lax.rem(tile // 2 - partner // 2 + TILE // 2, TILE // 2)
        out[s] = turned[place[behind] + lax.rem(partner + side, 2) * 17]
        return carry

    lax.fori_loop(0, out.shape[0], step, 0)


def body(waveforms, band_widths, pair_table):
    slots = pair_table.shape[1]
    bf16 = jnp.bfloat16
    scratch = [
        pltpu.SMEM((BAND,), jnp.int32),
        pltpu.VMEM(waveforms.shape, bf16),
        pltpu.VMEM((BINGROUPS * ROWS, SAMPLES), bf16),
        pltpu.VMEM((BINGROUPS, MSG, 128), bf16),
        pltpu.VMEM((2, BAND, MSG, 128), bf16),
        pltpu.VMEM((2, 17 * CH, WIDE // 2), bf16),
        pltpu.VMEM((GROUPS, 256, 256), bf16),
        pltpu.VMEM((2 * PART, GROUPS * 64), bf16),
        pltpu.VMEM((GROUPS * 64, 512), bf16),
        pltpu.VMEM((len(CHUNKS), 2, 4, PART, 128), bf16),
        pltpu.VMEM((len(CHUNKS), 4, PART, 128), bf16),
        pltpu.VMEM((len(CHUNKS), PART, 128), bf16),
        pltpu.VMEM((len(CHUNKS), 2, PART, 128), bf16),
        pltpu.VMEM((len(CHUNKS), 2, PART, 128), bf16),
        pltpu.VMEM((len(CHUNKS), PART, 128), bf16),
        pltpu.VMEM((len(CHUNKS), 2, PART, 128), bf16),
        pltpu.VMEM((PART, 512), bf16),
    ]
    dma = pltpu.SemaphoreType.DMA
    scratch += [
        dma((5,)),
        dma((12,)),
        dma((BAND,)),
        dma((BAND,)),
        dma((32,)),
        dma((32,)),
        dma((4 * len(CHUNKS),)),
        dma((4 * len(CHUNKS),)),
    ]
    vmem = pl.BlockSpec(memory_space=pltpu.VMEM)
    smem = pl.BlockSpec(memory_space=pltpu.SMEM)
    summed = pl.pallas_call(
        _main_kernel,
        out_shape=jax.ShapeDtypeStruct((34, 4, CH, LAGS), bf16),
        in_specs=[pl.BlockSpec(memory_space=pl.ANY)] * 5,
        out_specs=vmem,
        scratch_shapes=scratch,
        compiler_params=pltpu.CompilerParams(
            collective_id=0, has_side_effects=True, vmem_limit_bytes=60 * 1024 * 1024
        ),
        name="correlate",
    )(
        band_widths,
        waveforms,
        jnp.asarray(_forward_const()),
        jnp.asarray(_inverse_const()),
        jnp.asarray(_select_const()),
    )
    place = np.zeros((TILE // 2,), np.int32)
    for r, i in POS.items():
        place[r] = i
    placed = pl.pallas_call(
        _place_kernel,
        out_shape=jax.ShapeDtypeStruct((slots, 4, CH, LAGS), bf16),
        in_specs=[smem, smem, vmem],
        out_specs=vmem,
        name="place",
    )(pair_table, jnp.asarray(place), summed)
    return placed[None]


def solution(mesh):
    placed = (P("tile", "band", None), P(), P("tile", None))
    return jax.shard_map(
        body,
        mesh=mesh,
        in_specs=placed,
        out_specs=P("tile", None, "band", None, None),
        check_vma=False,
    )
```
